32 devices in a mesh: chain: 8 (over y, x, core), tp: 4 (over z).
Axes of the slice: x: 2, y: 2, z: 4, core: 2. Of those that a mesh axis runs over, the one named last changes fastest.
Arguments:
- tokens: bfloat16 [4096, 8192], P('chain', 'tp'), may hold values from -800 to 800
- gain: float32 [8192], replicated, may hold values from 0.6 to 5
- w_query: bfloat16 [8192, 8192], P(None, 'tp'), may hold values from -0.125 to 0.125
- key_value_weight: bfloat16 [8192, 2048], P(None, 'tp'), may hold values from -0.125 to 0.125
- offsets: int32 [8], P('chain'), may hold values from 0 to 4032, as said below
- lengths: int32 [4], replicated, may hold values from 1 to 4096, as said below
Outputs:
- context: bfloat16 [4096, 8192], P('chain', 'tp')
- decode_cache: bfloat16 [16384, 2048], P('chain', 'tp')
The draws below stay inside these ranges and needn't reach their ends.
Inputs may be any that keep to these rules, and one draw needn't show every extreme that they name: `offsets`: the first stretch starts at position 0, each later stretch starts at least 512 positions after the previous one, and the last one starts at (8 - 1) * 576. `lengths`: some decode group receives all 4096 tokens.
All inputs are finite; a program needn't handle non-finite values.
Results may differ from the reference program's by a relative error of at most 0.012.
The reference program's roundings to bfloat16 on the way count: a program that leaves them out, or rounds other values in their place, can miss the bound.
Values may be sent and summed in bfloat16 or wider, within the bound.
No kernel may reach another device: no remote copies, remote signals or barrier semaphores. Data moves between devices by JAX's collectives and lax.ppermute only.
A program may use at most 320 MiB of HBM per device.

```python
import jax
import jax.numpy as jnp
from jax import lax

MODEL_WIDTH = 8192
QUERY_HEADS = 64
KEY_VALUE_HEADS = 8
HEAD_SIZE = 128
STRETCH = 512
GROUPS = 4
GAP = 64
PROMPT_TOKENS = 4096
N_CHAIN = 8


def draw_tokens(key, part):
    first, second = jax.random.split(key, 2)
    column = jnp.arange(MODEL_WIDTH).astype(jnp.float32) / MODEL_WIDTH
    base = jnp.clip(jax.random.normal(first, (PROMPT_TOKENS, MODEL_WIDTH), jnp.float32), -4.0, 4.0)
    rows = jnp.exp(jax.random.uniform(second, (PROMPT_TOKENS, 1), jnp.float32, 0.0, jnp.log(10.0)))
    value_rows = base * rows * jnp.power(3.0, column)[None, :]
    return value_rows.astype(jnp.bfloat16)


def draw_gain(key, part):
    value_rows = jax.random.uniform(key, (MODEL_WIDTH,), jnp.float32, 0.6, 1.4)
    return value_rows


def draw_offsets(key, part):
    section = jnp.arange(N_CHAIN, dtype=jnp.int32)
    gaps = jax.random.randint(key, (N_CHAIN,), 0, GAP).astype(jnp.int32)
    gaps = jnp.where(section == 0, 0, gaps).astype(jnp.int32)
    starts = section * STRETCH + jnp.cumsum(gaps).astype(jnp.int32)
    final_start = jnp.int32((N_CHAIN - 1) * (STRETCH + GAP))
    return jnp.where(section == N_CHAIN - 1, final_start, starts).astype(jnp.int32)


def draw_lengths(key, part):
    first, second = jax.random.split(key)
    value_rows = jax.random.randint(first, (GROUPS,), 1, PROMPT_TOKENS + 1).astype(jnp.int32)
    chosen = jax.random.randint(second, (), 0, GROUPS)
    return jnp.where(jnp.arange(GROUPS) == chosen, PROMPT_TOKENS, value_rows).astype(jnp.int32)


def shard_levels(rng, dims, cuts, smallest, top_value):
    factor_of = 1.0
    for dim, shards_of in cuts:
        steps = jax.random.uniform(jax.random.fold_in(jax.random.fold_in(rng, 6), dim), (shards_of,), jnp.float32, smallest / len(cuts), top_value / len(cuts))
        factor_of = factor_of * jnp.repeat(jnp.exp(steps), dims[dim] // shards_of).reshape((-1,) + (1,) * (len(dims) - 1 - dim))
    return factor_of


def bell_draw(own_key, extent, width, bound, cuts=(), held_as=jnp.bfloat16):
    factor_of = shard_levels(own_key, extent, cuts, -0.22, 0.18) if cuts else 1.0
    entries = jax.random.normal(own_key, extent, jnp.float32) * width * factor_of
    return jnp.minimum(jnp.maximum(entries, -bound), bound).astype(held_as)


def setup_inputs(seed: int = 0) -> dict:
    key_of = jax.random.split(jax.random.key(seed), 7)
    return {
        "tokens": draw_tokens(jax.random.fold_in(key_of[6], 71), 0),
        "gain": draw_gain(jax.random.fold_in(key_of[6], 71), 0),
        "w_query": bell_draw(key_of[2], (MODEL_WIDTH, QUERY_HEADS * HEAD_SIZE), (MODEL_WIDTH // 4) ** -0.5, 0.125, ((1, 4),)),
        "key_value_weight": bell_draw(key_of[3], (MODEL_WIDTH, KEY_VALUE_HEADS * 2 * HEAD_SIZE), (MODEL_WIDTH // 4) ** -0.5, 0.125, ((1, 4),)),
        "offsets": draw_offsets(jax.random.fold_in(key_of[6], 71), 0),
        "lengths": draw_lengths(jax.random.fold_in(key_of[6], 71), 0),
    }


def rotary(vec, pos):
    half = vec.shape[-1] // 2
    freq = jnp.power(jnp.float32(500000.0), -2.0 * jnp.arange(half).astype(jnp.float32) / vec.shape[-1])
    angle = pos.astype(jnp.float32)[:, None] * freq[None, :]
    cosine = jnp.cos(angle)[:, None, :]
    sine = jnp.sin(angle)[:, None, :]
    first = vec[..., :half]
    second = vec[..., half:]
    return jnp.concatenate([first * cosine - second * sine, second * cosine + first * sine], axis=-1)

def reference(tokens, gain, w_query, key_value_weight, offsets, lengths):
    xf = tokens.astype(jnp.float32)
    inv_rms = lax.rsqrt(lax.optimization_barrier(jnp.mean(xf * xf, axis=1)) + 1e-05)
    normed = (xf * gain[None, :]).astype(jnp.bfloat16)
    query = jnp.dot(normed, w_query, preferred_element_type=jnp.float32) * inv_rms[:, None]
    key_value_pair = jnp.dot(normed, key_value_weight, preferred_element_type=jnp.float32) * inv_rms[:, None]
    position = (offsets[:, None] + jnp.arange(STRETCH, dtype=jnp.int32)[None, :]).reshape(PROMPT_TOKENS)
    rquery = rotary(query.reshape(PROMPT_TOKENS, QUERY_HEADS, HEAD_SIZE), position).astype(jnp.bfloat16)
    key_value_pair = key_value_pair.reshape(PROMPT_TOKENS, KEY_VALUE_HEADS, 2, HEAD_SIZE)
    rotated_keys = rotary(key_value_pair[:, :, 0], position).astype(jnp.bfloat16)
    value_rows = key_value_pair[:, :, 1].astype(jnp.bfloat16)
    query_group_ratio = QUERY_HEADS // KEY_VALUE_HEADS
    causal = jnp.arange(PROMPT_TOKENS)[None, :] <= jnp.arange(PROMPT_TOKENS)[:, None]
    scale = jnp.float32(1.0 / HEAD_SIZE ** 0.5)

    def one_head(head):
        kvh = head // query_group_ratio
        qh = jnp.take(rquery, head, axis=1)
        kh = jnp.take(rotated_keys, kvh, axis=1)
        vh = jnp.take(value_rows, kvh, axis=1)
        scores = jnp.dot(qh, kh.T, preferred_element_type=jnp.float32) * scale
        scores = jnp.where(causal, scores, jnp.float32(-1e+30))
        top = lax.optimization_barrier(jnp.max(scores, axis=1, keepdims=True))
        prob = jnp.where(causal, jnp.exp(scores - top), jnp.float32(0.0))
        total = lax.optimization_barrier(jnp.sum(prob, axis=1, keepdims=True))
        weights = prob.astype(jnp.bfloat16)
        return jnp.dot(weights, vh, preferred_element_type=jnp.float32) / total
    heads = lax.map(one_head, jnp.arange(QUERY_HEADS, dtype=jnp.int32))
    context = jnp.transpose(heads, (1, 0, 2)).reshape(PROMPT_TOKENS, QUERY_HEADS * HEAD_SIZE).astype(jnp.bfloat16)
    key_value_row = jnp.stack([rotated_keys, value_rows], axis=2).reshape(PROMPT_TOKENS, KEY_VALUE_HEADS * 2 * HEAD_SIZE)
    tindex = jnp.arange(PROMPT_TOKENS, dtype=jnp.int32)
    pieces = [jnp.where((tindex < lengths[g])[:, None], key_value_row, jnp.zeros_like(key_value_row)) for g in range(GROUPS)]
    decode_cache = jnp.concatenate(pieces, axis=0)
    return (context, decode_cache)
```

```python
import functools
import math

import jax
import jax.numpy as jnp
from jax import lax
from jax.experimental import pallas as pl
from jax.experimental.pallas import tpu as pltpu
from jax.sharding import PartitionSpec as P

HEAD_SIZE = 128
GROUPS = 4
TILE = 64
DEPTH = 512
KEYS = 512
VMEM = 56 * 1024 * 1024
LOW = -1e30


def shifted(x, axis, by):
    n = lax.axis_size(axis)
    return lax.ppermute(x, axis, [(i, (i + by) % n) for i in range(n)])


def paired(x, axis, mask):
    return lax.ppermute(x, axis, [(i, i ^ mask) for i in range(lax.axis_size(axis))])


def cut(x, start, rows, after):
    def body(x_ref, *refs):
        refs[-1][...] = x_ref[...]

    return pl.pallas_call(
        body,
        grid=(rows // TILE,),
        in_specs=[pl.BlockSpec((TILE, x.shape[1]), lambda i: (start // TILE + i, 0))]
        + [pl.BlockSpec(memory_space=pl.ANY)] * len(after),
        out_specs=pl.BlockSpec((TILE, x.shape[1]), lambda i: (i, 0)),
        out_shape=jax.ShapeDtypeStruct((rows, x.shape[1]), x.dtype),
    )(x, *after)


def project(parts, order, gain, weights, carry, tables, name):
    count = len(parts)
    rows = sum(p.shape[0] for p in parts[0])
    width = parts[0][0].shape[1]
    steps = width // DEPTH
    model = weights[0][0].shape[0]
    n_weights = len(weights)
    flat = [p for part in parts for p in part]

    def body(order_ref, *refs):
        refs = list(refs)
        part_refs = [[refs.pop(0) for _ in part] for part in parts]
        gain_ref = refs.pop(0)
        w_refs = [refs.pop(0) for _ in weights]
        carry_refs = [refs.pop(0) for _ in range(n_weights + 1)] if carry else None
        table_refs = [refs.pop(0) for _ in range(2)] if tables else None
        outs = [refs.pop(0) for _ in range(n_weights if tables else n_weights + 1)]
        x_ref = refs.pop(0)
        sums = refs if tables else outs
        step = pl.program_id(0)

        @pl.when(step == 0)
        def _():
            for i, s in enumerate(sums):
                s[...] = carry_refs[i][...] if carry else jnp.zeros_like(s)

        for i in range(count):

            @pl.when(step // steps == i)
            def _():
                at = 0
                for ref in part_refs[i]:
                    x_ref[at : at + ref.shape[0], :] = ref[...]
                    at += ref.shape[0]

        x = x_ref[...].astype(jnp.float32)
        normed = (x * gain_ref[0]).astype(jnp.bfloat16)
        square = x * x
        sums[-1][...] += sum(square[:, i : i + 128] for i in range(0, DEPTH, 128))
        for s, w in zip(sums, w_refs):
            s[...] += jnp.dot(normed, w[...], preferred_element_type=jnp.float32)

        if tables:

            @pl.when(step == count * steps - 1)
            def _():
                mean = jnp.sum(sums[-1][...], axis=1, keepdims=True) / model
                inv = lax.rsqrt(mean + 1e-05)
                cosine, sine = table_refs[0][...], table_refs[1][...]
                for s, out, (_, turned) in zip(sums, outs, weights):
                    for h, turn in enumerate(turned):
                        u = s[:, h * 128 : h * 128 + 128] * inv
                        if turn:
                            u = u * cosine + pltpu.roll(u, 64, 1) * sine
                        out[:, h * 128 : h * 128 + 128] = u.astype(jnp.bfloat16)

    def part_spec(i, p):
        return pl.BlockSpec(
            (p.shape[0], DEPTH), lambda s, order: (0, jnp.clip(s - i * steps, 0, steps - 1))
        )

    def block(s, order):
        return order[s // steps] * steps + s % steps

    def whole(a):
        return pl.BlockSpec(a.shape, lambda s, order: (0,) * len(a.shape))

    columns = [w.shape[1] for w, _ in weights]
    sum_shapes = [(rows, c) for c in columns] + [(rows, 128)]
    in_specs = [part_spec(i, p) for i, part in enumerate(parts) for p in part]
    in_specs += [pl.BlockSpec((1, 1, DEPTH), lambda s, order: (block(s, order), 0, 0))]
    in_specs += [
        pl.BlockSpec((DEPTH, c), lambda s, order: (block(s, order), 0)) for c in columns
    ]
    extra = list(carry or ()) + list(tables or ())
    in_specs += [whole(a) for a in extra]
    if tables:
        out_shape = [jax.ShapeDtypeStruct((rows, c), jnp.bfloat16) for c in columns]
        scratch = [pltpu.VMEM(s, jnp.float32) for s in sum_shapes]
    else:
        out_shape = [jax.ShapeDtypeStruct(s, jnp.float32) for s in sum_shapes]
        scratch = []
    moved = count * width * sum(columns) * 2
    return pl.pallas_call(
        body,
        grid_spec=pltpu.PrefetchScalarGridSpec(
            num_scalar_prefetch=1,
            grid=(count * steps,),
            in_specs=in_specs,
            out_specs=[whole(s) for s in out_shape],
            scratch_shapes=[pltpu.VMEM((rows, DEPTH), jnp.bfloat16)] + scratch,
        ),
        out_shape=out_shape,
        name=name,
        cost_estimate=pl.CostEstimate(
            flops=2 * rows * count * width * sum(columns), bytes_accessed=moved, transcendentals=0
        ),
        compiler_params=pltpu.CompilerParams(vmem_limit_bytes=VMEM),
    )(order, *flat, gain.reshape(model // DEPTH, 1, DEPTH), *[w for w, _ in weights], *extra)


def stacked(q_ref, ratio):
    return jnp.concatenate(
        [q_ref[:, h * HEAD_SIZE : (h + 1) * HEAD_SIZE] for h in range(ratio)], axis=0
    )


def scale():
    return math.log2(math.e) / math.sqrt(HEAD_SIZE)


def first_block(q, k, v, valid, state):
    s = lax.dot_general(q, k, (((1,), (1,)), ((), ())), preferred_element_type=jnp.float32)
    s = jnp.where(valid, s, LOW)
    top = jnp.max(s, axis=1, keepdims=True)
    p = jnp.exp2((s - top) * scale()).astype(jnp.bfloat16)
    fresh = jnp.dot(p, v, preferred_element_type=jnp.float32)
    keep_top(state, fresh, top)


def keep_top(state, sums, top):
    lane = lax.broadcasted_iota(jnp.int32, sums.shape, 1)
    state[...] = jnp.where(lane < HEAD_SIZE + 64, sums, top)


def next_block(q, kt, v, valid, state):
    s = jnp.dot(q, kt, preferred_element_type=jnp.float32)
    if valid is not None:
        s = jnp.where(valid, s, LOW)
    old = state[:, 2 * HEAD_SIZE - 1 :]
    top = jnp.maximum(old, jnp.max(s, axis=1, keepdims=True))
    p = jnp.exp2((s - top) * scale()).astype(jnp.bfloat16)
    fresh = state[...] * jnp.exp2((old - top) * scale())
    fresh += jnp.dot(p, v, preferred_element_type=jnp.float32)
    keep_top(state, fresh, top)


def over_keys(q, load, valid_count, state):
    full = valid_count // KEYS

    def one(i, _):
        kt, v = load(i)
        next_block(q, kt, v, None, state)
        return 0

    lax.fori_loop(0, full, one, 0)

    @pl.when(valid_count % KEYS > 0)
    def _():
        kt, v = load(full)
        column = lax.broadcasted_iota(jnp.int32, (q.shape[0], KEYS), 1)
        next_block(q, kt, v, column < valid_count - full * KEYS, state)


def with_ones(v):
    return jnp.concatenate([v, jnp.ones_like(v)], axis=1)


def attend_early(place, query, own, sets, state, start, rows, total_rows):
    kv_local = own.shape[1] // (2 * HEAD_SIZE)
    ratio = query.shape[1] // HEAD_SIZE // kv_local
    height = ratio * TILE
    n_sets = len(sets)

    def body(place_ref, q_ref, own_ref, *refs):
        set_refs = refs[:n_sets]
        out = refs[-1].at[0, 0]
        t, g = pl.program_id(0), pl.program_id(1)
        me = place_ref[0]
        q = stacked(q_ref, ratio)
        k, v = own_ref[:, :HEAD_SIZE], own_ref[:, HEAD_SIZE:]
        row = lax.broadcasted_iota(jnp.int32, (height, rows), 0) % TILE + t * TILE
        column = lax.broadcasted_iota(jnp.int32, (height, rows), 1)
        first_block(q, k, with_ones(v), column <= row, out)
        for ref, (_, set_rows) in zip(set_refs, sets):

            def load(i, ref=ref):
                at = pl.ds(pl.multiple_of(i * KEYS, KEYS), KEYS)
                return ref[at, :HEAD_SIZE].T, with_ones(ref[at, HEAD_SIZE:])

            over_keys(q, load, (me + 1) * set_rows, out)

    tiles = total_rows // TILE
    state_shape = jax.ShapeDtypeStruct((tiles, kv_local, height, 2 * HEAD_SIZE), jnp.float32)
    in_specs = [
        pl.BlockSpec((TILE, ratio * HEAD_SIZE), lambda t, g, place: (t, g)),
        pl.BlockSpec((rows, 2 * HEAD_SIZE), lambda t, g, place: (0, g)),
    ]
    in_specs += [
        pl.BlockSpec((s.shape[0], 2 * HEAD_SIZE), lambda t, g, place: (0, g)) for s, _ in sets
    ]
    args = [query, own] + [s for s, _ in sets]
    aliases = {}
    if state is not None:
        aliases = {1 + len(args): 0}
        in_specs.append(pl.BlockSpec(memory_space=pl.ANY))
        args.append(state)
    keys = sum(s.shape[0] for s, _ in sets) + rows
    return pl.pallas_call(
        body,
        grid_spec=pltpu.PrefetchScalarGridSpec(
            num_scalar_prefetch=1,
            grid=(rows // TILE, kv_local),
            in_specs=in_specs,
            out_specs=pl.BlockSpec(
                (1, 1, height, 2 * HEAD_SIZE), lambda t, g, place: (start // TILE + t, g, 0, 0)
            ),
        ),
        out_shape=state_shape,
        input_output_aliases=aliases,
        name=f"early_{start}",
        cost_estimate=pl.CostEstimate(
            flops=8 * keys * rows * query.shape[1],
            bytes_accessed=keys * 1024,
            transcendentals=0,
        ),
        compiler_params=pltpu.CompilerParams(vmem_limit_bytes=VMEM),
    )(place, *args)


def attend_late(place, queries, own, near, far, far_near, state, cache, start, total_rows, last):
    rows = own.shape[0]
    kv_width = own.shape[1]
    kv_local = kv_width // (2 * HEAD_SIZE)
    ratio = queries[0].shape[1] // HEAD_SIZE // kv_local
    height = ratio * TILE
    others = far.shape[0] // rows
    chain = 2 * others + 2
    n_keys = chain * rows
    tiles = (start + rows) // TILE
    firsts = []
    at = 0
    for q in queries:
        firsts.append(at)
        at += q.shape[0] // TILE

    def body(place_ref, *refs):
        refs = list(refs)
        q_refs = [refs.pop(0) for _ in queries]
        own_ref, near_ref, far_ref, far_near_ref, state_ref = [refs.pop(0) for _ in range(5)]
        if cache is not None:
            refs.pop(0)
        if last:
            out, cache_out, kv, kt_ref, v_ref, q_scr, st = refs
        else:
            out, cache_out, kv, kt_ref, v_ref, q_scr = refs
            st = out.at[0, 0]
        t, g = pl.program_id(0), pl.program_id(1)
        me, length, span = place_ref[0], place_ref[1], place_ref[2]

        @pl.when((t == 0) & (g == 0))
        def _():
            def put(stretch, value):
                kv[pl.ds(pl.multiple_of(stretch * rows, rows), rows), :] = value

            put(me, own_ref[...])
            put(me ^ 1, near_ref[...])
            for i in range(others):
                put(me ^ (2 * i + 2), far_ref[i * rows : (i + 1) * rows, :])
                put(me ^ (2 * i + 3), far_near_ref[i * rows : (i + 1) * rows, :])
            for h in range(kv_local):
                base = h * 2 * HEAD_SIZE
                for b in range(0, n_keys, KEYS):
                    kt_ref[h, b // KEYS] = kv[b : b + KEYS, base : base + HEAD_SIZE].T
                v_ref[h] = with_ones(kv[:, base + HEAD_SIZE : base + 2 * HEAD_SIZE])

        piece = jnp.minimum(t, rows // TILE - 1) * TILE
        for j in range(GROUPS):
            at = pl.multiple_of((span + j) * rows + piece, TILE)
            index = (span + j) * total_rows + start + piece
            index += lax.broadcasted_iota(jnp.int32, (TILE, kv_width), 0)
            value = kv[pl.ds(at, TILE), :]
            cache_out[j] = jnp.where(index < length, value, jnp.zeros_like(value))

        for i, ref in enumerate(q_refs):

            @pl.when((t >= firsts[i]) & (t < firsts[i] + queries[i].shape[0] // TILE))
            def _():
                q_scr[...] = stacked(ref, ratio)

        st[...] = state_ref[0, 0]

        def load(i):
            return kt_ref[g, i], v_ref[g, pl.ds(pl.multiple_of(i * KEYS, KEYS), KEYS), :]

        over_keys(q_scr[...], load, me * rows, st)
        if last:
            done = st[:, :HEAD_SIZE] / st[:, HEAD_SIZE : HEAD_SIZE + 1]
            for h in range(ratio):
                out[:, h * HEAD_SIZE : (h + 1) * HEAD_SIZE] = done[
                    h * TILE : (h + 1) * TILE
                ].astype(jnp.bfloat16)

    def whole(a):
        return pl.BlockSpec(a.shape, lambda t, g, place: (0,) * len(a.shape))

    def q_spec(i, q):
        n = q.shape[0] // TILE
        return pl.BlockSpec(
            (TILE, ratio * HEAD_SIZE),
            lambda t, g, place: (jnp.clip(t - firsts[i], 0, n - 1), g),
        )

    state_spec = pl.BlockSpec((1, 1, height, 2 * HEAD_SIZE), lambda t, g, place: (t, g, 0, 0))
    in_specs = [q_spec(i, q) for i, q in enumerate(queries)]
    in_specs += [whole(a) for a in (own, near, far, far_near)]
    in_specs += [state_spec]
    args = list(queries) + [own, near, far, far_near, state]
    aliases = {} if last else {len(args): 0}
    if cache is not None:
        in_specs.append(pl.BlockSpec(memory_space=pl.ANY))
        args.append(cache)
        aliases[len(args)] = 1
    pieces = rows // TILE
    cache_spec = pl.BlockSpec(
        (GROUPS, TILE, kv_width),
        lambda t, g, place: (0, start // TILE + jnp.minimum(t, pieces - 1), 0),
    )
    set_shape = jax.ShapeDtypeStruct((n_keys, kv_width), jnp.bfloat16)
    cache_shape = jax.ShapeDtypeStruct((GROUPS, total_rows, kv_width), jnp.bfloat16)
    if last:
        out_shape = [
            jax.ShapeDtypeStruct((total_rows, queries[0].shape[1]), jnp.bfloat16),
            cache_shape,
        ]
        out_specs = [
            pl.BlockSpec((TILE, ratio * HEAD_SIZE), lambda t, g, place: (t, g)),
            cache_spec,
        ]
        scratch = [pltpu.VMEM(set_shape.shape, jnp.bfloat16)]
    else:
        out_shape = [jax.ShapeDtypeStruct(state.shape, jnp.float32), cache_shape, set_shape]
        out_specs = [state_spec, cache_spec, whole(set_shape)]
        scratch = []
    scratch += [
        pltpu.VMEM((kv_local, n_keys // KEYS, HEAD_SIZE, KEYS), jnp.bfloat16),
        pltpu.VMEM((kv_local, n_keys, 2 * HEAD_SIZE), jnp.bfloat16),
        pltpu.VMEM((height, HEAD_SIZE), jnp.bfloat16),
    ]
    if last:
        scratch.append(pltpu.VMEM((height, 2 * HEAD_SIZE), jnp.float32))
    return pl.pallas_call(
        body,
        grid_spec=pltpu.PrefetchScalarGridSpec(
            num_scalar_prefetch=1,
            grid=(tiles, kv_local),
            in_specs=in_specs,
            out_specs=out_specs,
            scratch_shapes=scratch,
        ),
        out_shape=out_shape,
        input_output_aliases=aliases,
        name=f"late_{start}",
        cost_estimate=pl.CostEstimate(
            flops=8 * n_keys * (start + rows) * queries[0].shape[1],
            bytes_accessed=tiles * 2 * height * 4096,
            transcendentals=0,
        ),
        compiler_params=pltpu.CompilerParams(vmem_limit_bytes=VMEM),
    )(place, *args)


def exchange(x):
    near = paired(x, "chain", 1)
    far = [paired(x, "chain", mask) for mask in range(2, lax.axis_size("chain"), 2)]
    far = jnp.concatenate(far, axis=0)
    return near, far, paired(far, "chain", 1)


def local(tokens, gain, w_query, key_value_weight, offsets, lengths):
    rows = tokens.shape[0]
    kv_local = key_value_weight.shape[1] // (2 * HEAD_SIZE)
    me = lax.axis_index("chain")
    chain = lax.axis_size("chain")
    tp = lax.axis_size("tp")
    lane = lax.axis_index("tp")

    half = HEAD_SIZE // 2
    freq = jnp.power(
        jnp.float32(500000.0), -2.0 * jnp.arange(half).astype(jnp.float32) / HEAD_SIZE
    )
    position = offsets[0] + jnp.arange(rows, dtype=jnp.int32)
    angle = position.astype(jnp.float32)[:, None] * freq[None, :]
    cosine, sine = jnp.cos(angle), jnp.sin(angle)
    cosine = jnp.concatenate([cosine, cosine], axis=1)
    sine = jnp.concatenate([-sine, sine], axis=1)

    members = chain // GROUPS
    span = me % members * GROUPS
    length = jnp.sum(jnp.where(jnp.arange(GROUPS) == me // members, lengths, 0))
    place = jnp.stack([me, length, span]).astype(jnp.int32)

    sizes = [rows * 3 // 8, rows // 4, rows // 4, rows // 8]
    starts = [sum(sizes[:i]) for i in range(len(sizes))]
    q_weight = (w_query, [True] * (w_query.shape[1] // HEAD_SIZE))
    kv_weight = (key_value_weight, [True, False] * kv_local)

    queries, sets, arrived = [], [], []
    state = cache = None
    for r, (start, size) in enumerate(zip(starts, sizes)):
        last = r == len(sizes) - 1
        tables = (cosine[start : start + size], sine[start : start + size])
        chunk = cut(tokens, start, size, arrived[r - 2] if r >= 2 else ())
        if tp == 4:
            up, down = shifted(chunk, "tp", 1), shifted(chunk, "tp", -1)
            arrived.append((up, down))
            opposite = (shifted(up[: size // 2], "tp", 1), shifted(down[size // 2 :], "tp", -1))
            order = jnp.stack([lane, (lane + 3) % 4, (lane + 1) % 4, (lane + 2) % 4])
            order = order.astype(jnp.int32)
            parts = [(chunk,), (up,), (down,), opposite]
        else:
            gathered = lax.all_gather(chunk, "tp", axis=0)
            arrived.append((gathered,))
            order = jnp.arange(tp, dtype=jnp.int32)
            parts = [(gathered[i],) for i in range(tp)]
        if last and tp == 4:
            *carry, squares = project(
                parts[:3], order[:3], gain, [q_weight, kv_weight], None, None, f"most_{start}"
            )
            (kv,) = project(
                parts[3:], order[3:], gain, [kv_weight], (carry[1], squares), tables, f"kv_{start}"
            )
            (query,) = project(
                parts[3:], order[3:], gain, [q_weight], (carry[0], squares), tables, f"q_{start}"
            )
        else:
            query, kv = project(
                parts, order, gain, [q_weight, kv_weight], None, tables, f"all_{start}"
            )
        queries.append(query)
        near, far, far_near = exchange(kv)
        state = attend_early(place, query, kv, sets, state, start, size, rows)
        got = attend_late(
            place, queries, kv, near, far, far_near, state, cache, start, rows, last
        )
        if last:
            context, cache = got
        else:
            state, cache, ready = got
            sets.append((ready, size))
    return context, cache.reshape(GROUPS * rows, key_value_weight.shape[1])


def solution(mesh):
    in_specs = (P("chain", "tp"), P(), P(None, "tp"), P(None, "tp"), P("chain"), P())
    out_specs = (P("chain", "tp"), P("chain", "tp"))
    return jax.shard_map(local, mesh=mesh, in_specs=in_specs, out_specs=out_specs, check_vma=False)
```

```python
import math

import jax
import jax.numpy as jnp
from jax import lax
from jax.experimental import pallas as pl
from jax.experimental.pallas import tpu as pltpu
from jax.sharding import PartitionSpec as P

HEAD_SIZE = 128
GROUPS = 4
TILE = 64
FIRST = 4
KEYS = 448
SUMS = HEAD_SIZE + 16
VMEM = 63 * 1024 * 1024
SMALL = pl.CostEstimate(flops=1000, bytes_accessed=1000, transcendentals=0)
ANY = pl.BlockSpec(memory_space=pl.ANY)


def shifted(x, axis, by):
    n = lax.axis_size(axis)
    return lax.ppermute(x, axis, [(i, (i + by) % n) for i in range(n)])


def paired(x, axis, mask):
    return lax.ppermute(x, axis, [(i, i ^ mask) for i in range(lax.axis_size(axis))])


def cut(x, start, rows, after, name):
    def body(x_ref, *refs):
        out, held, sems = refs[-3:]
        for i, (a, b) in enumerate([(x_ref.at[pl.ds(start, rows), :], held), (held, out)]):
            copy = pltpu.make_async_copy(a, b, sems.at[i])
            copy.start()
            copy.wait()

    return pl.pallas_call(
        body,
        in_specs=[pl.BlockSpec(memory_space=pltpu.HBM)] + [ANY] * len(after),
        out_specs=pl.BlockSpec(memory_space=pltpu.HBM),
        out_shape=jax.ShapeDtypeStruct((rows, x.shape[1]), x.dtype),
        scratch_shapes=[
            pltpu.VMEM((rows, x.shape[1]), x.dtype),
            pltpu.SemaphoreType.DMA((2,)),
        ],
        cost_estimate=SMALL,
        name=name,
    )(x, *after)


def normed_rows(parts_refs, gain_ref, x_ref, square_ref):
    at = 0
    for ref in parts_refs:
        rows = slice(at, at + ref.shape[0])
        x = ref[...].astype(jnp.float32)
        x_ref[rows, :] = (x * gain_ref[0]).astype(jnp.bfloat16)
        square = x * x
        square_ref[rows, :] += sum(square[:, i : i + 128] for i in range(0, x.shape[1], 128))
        at += ref.shape[0]


def add_products(parts, order, gain, weights, carry, depth, after, name):
    count = len(parts)
    rows, width = parts[0].shape
    pieces = rows // TILE
    depth = min(depth, width)
    steps = width // depth
    model = weights[0].shape[0]
    n = len(weights)

    def body(order_ref, *refs):
        refs = list(refs)
        part_refs = [refs.pop(0) for _ in parts]
        gain_ref = refs.pop(0)
        w_refs = [refs.pop(0) for _ in weights]
        carry_refs = [[refs.pop(0) for _ in range(pieces)] for _ in range(n + 1)] if carry else None
        *sums, x_ref = refs[len(after) :]
        step = pl.program_id(0)

        @pl.when(step == 0)
        def _():
            for i, s in enumerate(sums):
                if carry:
                    for piece, ref in enumerate(carry_refs[i]):
                        s[piece * TILE : (piece + 1) * TILE, :] = ref[...]
                else:
                    s[...] = jnp.zeros_like(s)

        for i in range(count):

            @pl.when(step // steps == i)
            def _():
                normed_rows([part_refs[i]], gain_ref, x_ref, sums[-1])

        for s, w in zip(sums, w_refs):
            s[...] += jnp.dot(x_ref[...], w[...], preferred_element_type=jnp.float32)

    def part_spec(i):
        return pl.BlockSpec(
            (rows, depth), lambda s, order: (0, jnp.clip(s - i * steps, 0, steps - 1))
        )

    def carry_spec(columns, piece):
        return pl.BlockSpec((TILE, columns), lambda s, order: (carry[1] // TILE + piece, 0))

    def block(s, order):
        return order[s // steps] * steps + s % steps

    columns = [w.shape[1] for w in weights]
    out_shape = [jax.ShapeDtypeStruct((rows, c), jnp.float32) for c in (*columns, 128)]
    in_specs = [part_spec(i) for i in range(count)]
    in_specs += [pl.BlockSpec((1, 1, depth), lambda s, order: (block(s, order), 0, 0))]
    in_specs += [
        pl.BlockSpec((depth, c), lambda s, order: (block(s, order), 0)) for c in columns
    ]
    if carry:
        in_specs += [carry_spec(s.shape[1], p) for s in out_shape for p in range(pieces)]
    return pl.pallas_call(
        body,
        grid_spec=pltpu.PrefetchScalarGridSpec(
            num_scalar_prefetch=1,
            grid=(count * steps,),
            in_specs=in_specs + [ANY] * len(after),
            out_specs=[pl.BlockSpec(s.shape, lambda s, order: (0, 0)) for s in out_shape],
            scratch_shapes=[pltpu.VMEM((rows, depth), jnp.bfloat16)],
        ),
        out_shape=out_shape,
        name=name,
        cost_estimate=SMALL,
        compiler_params=pltpu.CompilerParams(vmem_limit_bytes=VMEM),
    )(
        order,
        *parts,
        gain.reshape(model // depth, 1, depth),
        *weights,
        *([a for a in carry[0] for _ in range(pieces)] if carry else ()),
        *after,
    )


def finish_products(part, order, gain, weight, turned, sums, squares, tables, after, name):
    width = part[0].shape[1]
    rows = sum(p.shape[0] for p in part)
    model, columns = weight.shape
    wide = min(columns, 512)

    def body(order_ref, *refs):
        refs = list(refs)
        part_refs = [refs.pop(0) for _ in part]
        gain_ref, w_ref, sums_ref, squares_ref, cosine_ref, sine_ref = refs[:6]
        out, x_ref, square_ref = refs[-3:]

        @pl.when(pl.program_id(0) == 0)
        def _():
            square_ref[...] = squares_ref[...]
            normed_rows(part_refs, gain_ref, x_ref, square_ref)
            total = jnp.sum(square_ref[...], axis=1, keepdims=True)
            square_ref[...] = jnp.broadcast_to(lax.rsqrt(total / model + 1e-05), square_ref.shape)

        inv = square_ref[...]
        sums = sums_ref[...] + jnp.dot(x_ref[...], w_ref[...], preferred_element_type=jnp.float32)
        for i, at in enumerate(range(0, wide, 128)):
            u = sums[:, at : at + 128] * inv
            if turned[i % 2]:
                u = u * cosine_ref[...] + pltpu.roll(u, 64, 1) * sine_ref[...]
            out[:, at : at + 128] = u.astype(jnp.bfloat16)

    def whole(a):
        return pl.BlockSpec(a.shape, lambda s, order: (0, 0))

    by_columns = pl.BlockSpec((rows, wide), lambda s, order: (0, s))
    return pl.pallas_call(
        body,
        grid_spec=pltpu.PrefetchScalarGridSpec(
            num_scalar_prefetch=1,
            grid=(columns // wide,),
            in_specs=[whole(p) for p in part]
            + [pl.BlockSpec((1, 1, width), lambda s, order: (order[0], 0, 0))]
            + [pl.BlockSpec((width, wide), lambda s, order: (order[0], s))]
            + [by_columns, whole(squares), whole(tables[0]), whole(tables[1])]
            + [ANY] * len(after),
            out_specs=by_columns,
            scratch_shapes=[
                pltpu.VMEM((rows, width), jnp.bfloat16),
                pltpu.VMEM((rows, 128), jnp.float32),
            ],
        ),
        out_shape=jax.ShapeDtypeStruct((rows, columns), jnp.bfloat16),
        name=name,
        cost_estimate=SMALL,
        compiler_params=pltpu.CompilerParams(vmem_limit_bytes=VMEM),
    )(order, *part, gain.reshape(model // width, 1, width), weight, sums, squares, *tables, *after)


def stacked(q_ref, tile, ratio, group=0):
    rows = slice(tile * TILE, (tile + 1) * TILE)
    heads = range(group * ratio, (group + 1) * ratio)
    return jnp.concatenate(
        [q_ref[rows, h * HEAD_SIZE : (h + 1) * HEAD_SIZE] for h in heads], axis=0
    )


def scores(k, q):
    return lax.dot_general(k, q, (((1,), (1,)), ((), ())), preferred_element_type=jnp.float32)


def fold(s, vt, state, at, first=False):
    scale = math.log2(math.e) / math.sqrt(HEAD_SIZE)
    live = HEAD_SIZE + 8
    top = jnp.max(s, axis=0, keepdims=True)
    if not first:
        old = state[live : live + 1, at]
        top = jnp.maximum(old, top)
    p = jnp.exp2((s - top) * scale).astype(jnp.bfloat16)
    fresh = jnp.dot(vt, p, preferred_element_type=jnp.float32)[:live]
    if not first:
        fresh += state[:live, at] * jnp.exp2((old - top) * scale)
    state[:live, at] = fresh
    state[live : live + 1, at] = top


def fold_all(blocks):
    work = [(k, vt, *tile) for k, vt, tiles in blocks for tile in tiles]
    ahead = scores(work[0][0], work[0][2]())
    for i, (_, vt, _, state, at) in enumerate(work):
        s = ahead
        if i + 1 < len(work):
            ahead = scores(work[i + 1][0], work[i + 1][2]())
        fold(s, vt, state, at)


def values_and_ones(v, count=None):
    if count is not None:
        row = lax.broadcasted_iota(jnp.int32, v.shape, 0)
        v = jnp.where(row < count, v, jnp.zeros_like(v))
    n = v.shape[0]
    lane = lax.broadcasted_iota(jnp.int32, (SUMS - HEAD_SIZE, n), 1)
    row = lax.broadcasted_iota(jnp.int32, (SUMS - HEAD_SIZE, n), 0)
    live = row < 8
    if count is not None:
        live = live & (lane < count)
    ones = jnp.where(live, 1.0, 0.0).astype(jnp.bfloat16)
    return jnp.concatenate([v.T, ones], axis=0)


def attend_early(place, query, own, sets, after, name):
    rows = query.shape[0]
    kv_local = own[0].shape[1] // (2 * HEAD_SIZE)
    ratio = query.shape[1] // HEAD_SIZE // kv_local
    wide = ratio * TILE
    count = rows // TILE

    def body(place_ref, q_ref, *refs):
        own_refs = refs[: len(own)]
        set_refs = refs[len(own) : len(own) + 2 * len(sets)]
        out = refs[-1]
        me = place_ref[0]
        groups = [
            [
                (
                    lambda t=t, g=g: stacked(q_ref, t, ratio, g),
                    out.at[g],
                    slice(t * wide, (t + 1) * wide),
                )
                for t in range(count)
            ]
            for g in range(kv_local)
        ]

        def own_block(ref, g):
            at = g * 2 * HEAD_SIZE
            v = ref[:, at + HEAD_SIZE : at + 2 * HEAD_SIZE]
            return ref[:, at : at + HEAD_SIZE], values_and_ones(v)

        for g, tiles in enumerate(groups):
            k, vt = own_block(own_refs[-1], g)
            for t, (q, state, at) in enumerate(tiles):
                upto = (t + 1) * TILE
                column = lax.broadcasted_iota(jnp.int32, (upto, wide), 1) % TILE + t * TILE
                key = lax.broadcasted_iota(jnp.int32, (upto, wide), 0)
                s = jnp.where(key <= column, scores(k[:upto], q()), -1e30)
                fold(s, vt[:, :upto], state, at, first=True)
        for ref in own_refs[:-1]:
            fold_all([(*own_block(ref, g), tiles) for g, tiles in enumerate(groups)])
        for i, (_, _, set_rows) in enumerate(sets):
            k_ref, vt_ref = set_refs[2 * i], set_refs[2 * i + 1]

            def one(b, _):
                at = pl.ds(pl.multiple_of(b * KEYS, 64), KEYS)
                fold_all([(k_ref[g, at, :], vt_ref[g, b], tiles) for g, tiles in enumerate(groups)])
                return 0

            lax.fori_loop(0, (me * set_rows + KEYS - 1) // KEYS, one, 0)

    def whole(a):
        return pl.BlockSpec(a.shape, lambda i, place: (0,) * len(a.shape))

    args = [query, *own, *[a for s in sets for a in s[:2]]]
    state_shape = jax.ShapeDtypeStruct((kv_local, SUMS, count * wide), jnp.float32)
    return pl.pallas_call(
        body,
        grid_spec=pltpu.PrefetchScalarGridSpec(
            num_scalar_prefetch=1,
            grid=(1,),
            in_specs=[whole(a) for a in args] + [ANY] * len(after),
            out_specs=whole(state_shape),
        ),
        out_shape=state_shape,
        name=name,
        cost_estimate=SMALL,
        compiler_params=pltpu.CompilerParams(vmem_limit_bytes=VMEM),
    )(place, *args, *after)


def attend_late(place, queries, states, arrived, rows, cache, start, total, last, after):
    kv_width = arrived[0].shape[1]
    kv_local = kv_width // (2 * HEAD_SIZE)
    ratio = queries[0].shape[1] // HEAD_SIZE // kv_local
    wide = ratio * TILE
    n_keys = sum(a.shape[0] for a in arrived)
    blocks = -(-n_keys // KEYS)
    n = len(queries)
    n_cache = 0 if cache is None else 1

    def body(place_ref, *refs):
        refs = list(refs)
        q_refs = [refs.pop(0) for _ in queries]
        state_refs = [refs.pop(0).at[0] for _ in states]
        arrived_refs = [refs.pop(0) for _ in arrived]
        for _ in range(n_cache + len(after)):
            refs.pop(0)
        cache_ref = refs.pop(0)
        if last:
            out = refs.pop(0)
            k_ref, vt_ref, kv, piece, sems, *work = refs
        else:
            work = [refs.pop(0).at[0] for _ in states]
            k_out, vt_out = refs.pop(0), refs.pop(0)
            k_ref, vt_ref, kv, piece, sems = refs
        g = pl.program_id(0)
        me, length, span = place_ref[0], place_ref[1], place_ref[2]
        count = me * rows

        def copies():
            return [
                pltpu.make_async_copy(
                    piece.at[j], cache_ref.at[j, pl.ds(start, rows), :], sems.at[j]
                )
                for j in range(GROUPS)
            ]

        @pl.when(g == 0)
        def _():
            def put(stretch, value):
                kv[pl.ds(pl.multiple_of(stretch * rows, 64), rows), :] = value

            if len(arrived) == 1:
                kv[:n_keys, :] = arrived_refs[0][...]
            else:
                for j, ref in enumerate(arrived_refs):
                    for i in range(n_keys // rows // 2):
                        put(me ^ (2 * i + j), ref[i * rows : (i + 1) * rows, :])
            for j in range(GROUPS):
                value = kv[pl.ds(pl.multiple_of((span + j) * rows, 64), rows), :]
                index = (span + j) * total + start
                index += lax.broadcasted_iota(jnp.int32, value.shape, 0)
                piece[j] = jnp.where(index < length, value, jnp.zeros_like(value))
            for c in copies():
                c.start()
            for h in range(kv_local):
                base = h * 2 * HEAD_SIZE
                for b in range(blocks):
                    k = kv[b * KEYS : (b + 1) * KEYS, base : base + HEAD_SIZE]
                    row = lax.broadcasted_iota(jnp.int32, k.shape, 0) + b * KEYS
                    stand_in = jnp.broadcast_to(kv[0:16, base : base + HEAD_SIZE][:1], k.shape)
                    k_ref[h, b * KEYS : (b + 1) * KEYS, :] = jnp.where(row < count, k, stand_in)
                    v = kv[b * KEYS : (b + 1) * KEYS, base + HEAD_SIZE : base + 2 * HEAD_SIZE]
                    vt_ref[h, b] = values_and_ones(v, count - b * KEYS)

        for s, w in zip(state_refs, work):
            w[...] = s[...]
        tiles = [
            (lambda ref=ref, t=t: stacked(ref, t, ratio), w, slice(t * wide, (t + 1) * wide))
            for ref, w in zip(q_refs, work)
            for t in range(ref.shape[0] // TILE)
        ]

        def one(b, _):
            k = k_ref[g, pl.ds(pl.multiple_of(b * KEYS, 64), KEYS), :]
            fold_all([(k, vt_ref[g, b], tiles)])
            return 0

        lax.fori_loop(0, (count + KEYS - 1) // KEYS, one, 0)
        if last:
            for i, (_, w, at) in enumerate(tiles):
                done = (w[:HEAD_SIZE, at] / w[HEAD_SIZE : HEAD_SIZE + 1, at]).T
                for h in range(ratio):
                    out[i * TILE : (i + 1) * TILE, h * HEAD_SIZE : (h + 1) * HEAD_SIZE] = done[
                        h * TILE : (h + 1) * TILE
                    ].astype(jnp.bfloat16)
        else:
            k_out[0] = k_ref[g]
            vt_out[0] = vt_ref[g]

        @pl.when(g == kv_local - 1)
        def _():
            for c in copies():
                c.wait()

    def whole(a):
        return pl.BlockSpec(a.shape, lambda g, place: (0,) * len(a.shape))

    def by_group(a):
        return pl.BlockSpec((1,) + a.shape[1:], lambda g, place: (g,) + (0,) * (len(a.shape) - 1))

    k_shape = jax.ShapeDtypeStruct((kv_local, blocks * KEYS, HEAD_SIZE), jnp.bfloat16)
    vt_shape = jax.ShapeDtypeStruct((kv_local, blocks, SUMS, KEYS), jnp.bfloat16)
    cache_shape = jax.ShapeDtypeStruct((GROUPS, total, kv_width), jnp.bfloat16)
    args = [*queries, *states, *arrived]
    in_specs = [pl.BlockSpec((q.shape[0], ratio * HEAD_SIZE), lambda g, place: (0, g)) for q in queries]
    in_specs += [by_group(s) for s in states] + [whole(a) for a in arrived]
    aliases = {}
    if cache is not None:
        args.append(cache)
        in_specs.append(ANY)
        aliases[len(args)] = 0
    scratch = [
        pltpu.VMEM(k_shape.shape, jnp.bfloat16),
        pltpu.VMEM(vt_shape.shape, jnp.bfloat16),
        pltpu.VMEM((blocks * KEYS, kv_width), jnp.bfloat16),
        pltpu.VMEM((GROUPS, rows, kv_width), jnp.bfloat16),
        pltpu.SemaphoreType.DMA((GROUPS,)),
    ]
    if last:
        out_shape = [cache_shape, jax.ShapeDtypeStruct((total, queries[0].shape[1]), jnp.bfloat16)]
        out_specs = [ANY, pl.BlockSpec((total, ratio * HEAD_SIZE), lambda g, place: (0, g))]
        scratch += [pltpu.VMEM(s.shape[1:], jnp.float32) for s in states]
    else:
        out_shape = [cache_shape, *[jax.ShapeDtypeStruct(s.shape, s.dtype) for s in states]]
        out_shape += [k_shape, vt_shape]
        out_specs = [ANY] + [by_group(s) for s in out_shape[1:]]
        for i in range(n):
            aliases[1 + n + i] = 1 + i
    return pl.pallas_call(
        body,
        grid_spec=pltpu.PrefetchScalarGridSpec(
            num_scalar_prefetch=1,
            grid=(kv_local,),
            in_specs=in_specs + [ANY] * len(after),
            out_specs=out_specs,
            scratch_shapes=scratch,
        ),
        out_shape=out_shape,
        input_output_aliases=aliases,
        name=f"late_{start}",
        cost_estimate=SMALL,
        compiler_params=pltpu.CompilerParams(vmem_limit_bytes=VMEM),
    )(place, *args, *after)


def pack(blocks, after, name):
    rows = blocks[0].shape[0]

    def body(*refs):
        for i in range(len(blocks)):
            refs[-1][i * rows : (i + 1) * rows, :] = refs[i][...]

    spec = pl.BlockSpec(memory_space=pltpu.VMEM)
    shape = (rows * len(blocks), blocks[0].shape[1])
    return pl.pallas_call(
        body,
        in_specs=[spec] * len(blocks) + [ANY] * len(after),
        out_specs=spec,
        out_shape=jax.ShapeDtypeStruct(shape, blocks[0].dtype),
        cost_estimate=SMALL,
        name=name,
    )(*blocks, *after)


def exchange(x, after, name):
    even = [x] + [paired(x, "chain", mask) for mask in range(2, lax.axis_size("chain"), 2)]
    even = pack(even, after, name)
    return even, paired(even, "chain", 1)


def local(tokens, gain, w_query, key_value_weight, offsets, lengths):
    rows = tokens.shape[0]
    kv_local = key_value_weight.shape[1] // (2 * HEAD_SIZE)
    me = lax.axis_index("chain")
    chain = lax.axis_size("chain")
    tp = lax.axis_size("tp")
    lane = lax.axis_index("tp")

    half = HEAD_SIZE // 2
    freq = jnp.power(
        jnp.float32(500000.0), -2.0 * jnp.arange(half).astype(jnp.float32) / HEAD_SIZE
    )
    position = offsets[0] + jnp.arange(rows, dtype=jnp.int32)
    angle = position.astype(jnp.float32)[:, None] * freq[None, :]
    cosine, sine = jnp.cos(angle), jnp.sin(angle)
    cosine = jnp.concatenate([cosine, cosine], axis=1)
    sine = jnp.concatenate([-sine, sine], axis=1)

    members = chain // GROUPS
    span = me % members * GROUPS
    length = jnp.sum(jnp.where(jnp.arange(GROUPS) == me // members, lengths, 0))
    place = jnp.stack([me, length, span]).astype(jnp.int32)

    sizes = [rows * FIRST // 8, rows * (8 - FIRST) // 8]
    starts = [0, sizes[0]]
    weights = (w_query, key_value_weight)
    arrived = [None] * len(sizes)

    def send(r, after):
        chunk = cut(tokens, starts[r], sizes[r], after, f"cut_{r}")
        if tp == 4:
            arrived[r] = [chunk, shifted(chunk, "tp", 1), shifted(chunk, "tp", -1)]
        else:
            arrived[r] = [lax.all_gather(chunk, "tp", axis=0)]
        return chunk

    def forward(r, i, after):
        if tp != 4:
            return arrived[r][0]
        half = sizes[r] // 2
        part = cut(arrived[r][i], (i - 1) * half, half, after, f"pass_{r}_{i}")
        arrived[r].append(shifted(part, "tp", 3 - 2 * i))
        return part

    def near(r, after):
        if tp == 4:
            parts, which, carry = arrived[r][1:3], order[1:3], (own, starts[r])
        else:
            parts, which, carry = [arrived[r][0][i] for i in range(tp - 1)], order[:-1], None
        return add_products(parts, which, gain, weights, carry, 1024, after, f"near_{r}")

    def finish(r, weight, turned, sums, squares, after, name):
        part = arrived[r][3:] if tp == 4 else [arrived[r][0][tp - 1]]
        at = slice(starts[r], starts[r] + sizes[r])
        tables = (cosine[at], sine[at])
        return finish_products(
            part, order[-1:], gain, weight, turned, sums, squares, tables, after, f"{name}_{r}"
        )

    def keys_and_queries(r, sums):
        q_sums, kv_sums, squares = sums
        kv = finish(r, key_value_weight, (True, False), kv_sums, squares, (), "kv")
        query = finish(r, w_query, (True, True), q_sums, squares, (kv,), "query")
        return kv, query

    if tp == 4:
        order = jnp.stack([lane, (lane + 3) % 4, (lane + 1) % 4, (lane + 2) % 4])
        order = order.astype(jnp.int32)
    else:
        order = jnp.arange(tp, dtype=jnp.int32)

    step = send(0, ())
    if tp == 4:
        own = add_products([tokens], order[:1], gain, weights, None, 1024, (step,), "own")
        step = own[-1]
    step = forward(0, 1, (step,))
    step = forward(0, 2, (step,))
    step = send(1, (step,))
    sums = near(0, (step,))
    kv_0, query_0 = keys_and_queries(0, sums)
    keys = exchange(kv_0, (query_0,), "pack_0")
    state_0 = attend_early(place, query_0, [kv_0], [], keys[:1], "early_0")
    step = forward(1, 1, (state_0,))
    cache, state_0, k, vt = attend_late(
        place, [query_0], [state_0], keys, sizes[0], None, 0, rows, False, (step,)
    )
    step = forward(1, 2, (k,))
    sums = near(1, (step,))
    kv_1, query_1 = keys_and_queries(1, sums)
    keys = exchange(kv_1, (query_1,), "pack_1")
    sets = [(k, vt, sizes[0])]
    state_1 = attend_early(place, query_1, [kv_0, kv_1], sets, keys[:1], "early_1")
    queries, states = [query_0, query_1], [state_0, state_1]
    cache, context = attend_late(
        place, queries, states, keys, sizes[1], cache, starts[1], rows, True, ()
    )
    return context, cache.reshape(GROUPS * rows, key_value_weight.shape[1])


def solution(mesh):
    in_specs = (P("chain", "tp"), P(), P(None, "tp"), P(None, "tp"), P("chain"), P())
    out_specs = (P("chain", "tp"), P("chain", "tp"))
    return jax.shard_map(local, mesh=mesh, in_specs=in_specs, out_specs=out_specs, check_vma=False)
```

```python
import math

import jax
import jax.numpy as jnp
from jax import lax
from jax.experimental import pallas as pl
from jax.experimental.pallas import tpu as pltpu
from jax.sharding import PartitionSpec as P

HEAD_SIZE = 128
GROUPS = 4
TILE = 64
FIRST = 4
SUMS = HEAD_SIZE + 16
VMEM = 63 * 1024 * 1024
SMALL = pl.CostEstimate(flops=1000, bytes_accessed=1000, transcendentals=0)
ANY = pl.BlockSpec(memory_space=pl.ANY)


def shifted(x, axis, by):
    n = lax.axis_size(axis)
    return lax.ppermute(x, axis, [(i, (i + by) % n) for i in range(n)])


def paired(x, axis, mask):
    return lax.ppermute(x, axis, [(i, i ^ mask) for i in range(lax.axis_size(axis))])


def cut(x, start, rows, after, name):
    def body(x_ref, *refs):
        out, held, sems = refs[-3:]
        for i, (a, b) in enumerate([(x_ref.at[pl.ds(start, rows), :], held), (held, out)]):
            copy = pltpu.make_async_copy(a, b, sems.at[i])
            copy.start()
            copy.wait()

    return pl.pallas_call(
        body,
        in_specs=[pl.BlockSpec(memory_space=pltpu.HBM)] + [ANY] * len(after),
        out_specs=pl.BlockSpec(memory_space=pltpu.HBM),
        out_shape=jax.ShapeDtypeStruct((rows, x.shape[1]), x.dtype),
        scratch_shapes=[
            pltpu.VMEM((rows, x.shape[1]), x.dtype),
            pltpu.SemaphoreType.DMA((2,)),
        ],
        cost_estimate=SMALL,
        name=name,
    )(x, *after)


def normed_rows(parts_refs, gain_ref, x_ref, square_ref):
    at = 0
    for ref in parts_refs:
        rows = slice(at, at + ref.shape[0])
        x = ref[...].astype(jnp.float32)
        x_ref[rows, :] = (x * gain_ref[0]).astype(jnp.bfloat16)
        square = x * x
        square_ref[rows, :] += sum(square[:, i : i + 128] for i in range(0, x.shape[1], 128))
        at += ref.shape[0]


def add_products(parts, order, gain, weights, carry, depth, after, name):
    count = len(parts)
    rows, width = parts[0].shape
    pieces = rows // TILE
    depth = min(depth, width)
    steps = width // depth
    model = weights[0].shape[0]
    n = len(weights)

    def body(order_ref, *refs):
        refs = list(refs)
        part_refs = [refs.pop(0) for _ in parts]
        gain_ref = refs.pop(0)
        w_refs = [refs.pop(0) for _ in weights]
        carry_refs = [[refs.pop(0) for _ in range(pieces)] for _ in range(n + 1)] if carry else None
        *sums, x_ref = refs[len(after) :]
        step = pl.program_id(0)

        @pl.when(step == 0)
        def _():
            for i, s in enumerate(sums):
                if carry:
                    for piece, ref in enumerate(carry_refs[i]):
                        s[piece * TILE : (piece + 1) * TILE, :] = ref[...]
                else:
                    s[...] = jnp.zeros_like(s)

        for i in range(count):

            @pl.when(step // steps == i)
            def _():
                normed_rows([part_refs[i]], gain_ref, x_ref, sums[-1])

        for s, w in zip(sums, w_refs):
            s[...] += jnp.dot(x_ref[...], w[...], preferred_element_type=jnp.float32)

    def part_spec(i):
        return pl.BlockSpec(
            (rows, depth), lambda s, order: (0, jnp.clip(s - i * steps, 0, steps - 1))
        )

    def carry_spec(columns, piece):
        return pl.BlockSpec((TILE, columns), lambda s, order: (carry[1] // TILE + piece, 0))

    def block(s, order):
        return order[s // steps] * steps + s % steps

    columns = [w.shape[1] for w in weights]
    out_shape = [jax.ShapeDtypeStruct((rows, c), jnp.float32) for c in (*columns, 128)]
    in_specs = [part_spec(i) for i in range(count)]
    in_specs += [pl.BlockSpec((1, 1, depth), lambda s, order: (block(s, order), 0, 0))]
    in_specs += [
        pl.BlockSpec((depth, c), lambda s, order: (block(s, order), 0)) for c in columns
    ]
    if carry:
        in_specs += [carry_spec(s.shape[1], p) for s in out_shape for p in range(pieces)]
    return pl.pallas_call(
        body,
        grid_spec=pltpu.PrefetchScalarGridSpec(
            num_scalar_prefetch=1,
            grid=(count * steps,),
            in_specs=in_specs + [ANY] * len(after),
            out_specs=[pl.BlockSpec(s.shape, lambda s, order: (0, 0)) for s in out_shape],
            scratch_shapes=[pltpu.VMEM((rows, depth), jnp.bfloat16)],
        ),
        out_shape=out_shape,
        name=name,
        cost_estimate=SMALL,
        compiler_params=pltpu.CompilerParams(vmem_limit_bytes=VMEM),
    )(
        order,
        *parts,
        gain.reshape(model // depth, 1, depth),
        *weights,
        *([a for a in carry[0] for _ in range(pieces)] if carry else ()),
        *after,
    )


def finish_products(part, order, gain, weight, turned, sums, squares, tables, after, name):
    width = part[0].shape[1]
    rows = sum(p.shape[0] for p in part)
    model, columns = weight.shape
    wide = min(columns, 512)

    def body(order_ref, *refs):
        refs = list(refs)
        part_refs = [refs.pop(0) for _ in part]
        gain_ref, w_ref, sums_ref, squares_ref, cosine_ref, sine_ref = refs[:6]
        out, x_ref, square_ref = refs[-3:]

        @pl.when(pl.program_id(0) == 0)
        def _():
            square_ref[...] = squares_ref[...]
            normed_rows(part_refs, gain_ref, x_ref, square_ref)
            total = jnp.sum(square_ref[...], axis=1, keepdims=True)
            square_ref[...] = jnp.broadcast_to(lax.rsqrt(total / model + 1e-05), square_ref.shape)

        inv = square_ref[...]
        sums = sums_ref[...] + jnp.dot(x_ref[...], w_ref[...], preferred_element_type=jnp.float32)
        for i, at in enumerate(range(0, wide, 128)):
            u = sums[:, at : at + 128] * inv
            if turned[i % 2]:
                u = u * cosine_ref[...] + pltpu.roll(u, 64, 1) * sine_ref[...]
            out[:, at : at + 128] = u.astype(jnp.bfloat16)

    def whole(a):
        return pl.BlockSpec(a.shape, lambda s, order: (0, 0))

    by_columns = pl.BlockSpec((rows, wide), lambda s, order: (0, s))
    return pl.pallas_call(
        body,
        grid_spec=pltpu.PrefetchScalarGridSpec(
            num_scalar_prefetch=1,
            grid=(columns // wide,),
            in_specs=[whole(p) for p in part]
            + [pl.BlockSpec((1, 1, width), lambda s, order: (order[0], 0, 0))]
            + [pl.BlockSpec((width, wide), lambda s, order: (order[0], s))]
            + [by_columns, whole(squares), whole(tables[0]), whole(tables[1])]
            + [ANY] * len(after),
            out_specs=by_columns,
            scratch_shapes=[
                pltpu.VMEM((rows, width), jnp.bfloat16),
                pltpu.VMEM((rows, 128), jnp.float32),
            ],
        ),
        out_shape=jax.ShapeDtypeStruct((rows, columns), jnp.bfloat16),
        name=name,
        cost_estimate=SMALL,
        compiler_params=pltpu.CompilerParams(vmem_limit_bytes=VMEM),
    )(order, *part, gain.reshape(model // width, 1, width), weight, sums, squares, *tables, *after)


def stacked(q_ref, tile, ratio, group=0):
    rows = slice(tile * TILE, (tile + 1) * TILE)
    heads = range(group * ratio, (group + 1) * ratio)
    return jnp.concatenate(
        [q_ref[rows, h * HEAD_SIZE : (h + 1) * HEAD_SIZE] for h in heads], axis=0
    )


def scores(k, q):
    return lax.dot_general(k, q, (((1,), (1,)), ((), ())), preferred_element_type=jnp.float32)


def fold(s, vt, state, at, first=False):
    scale = math.log2(math.e) / math.sqrt(HEAD_SIZE)
    live = HEAD_SIZE + 8
    top = jnp.max(s, axis=0, keepdims=True)
    if not first:
        old = state[live : live + 1, at]
        top = jnp.maximum(old, top)
    p = jnp.exp2((s - top) * scale).astype(jnp.bfloat16)
    fresh = jnp.dot(vt, p, preferred_element_type=jnp.float32)[:live]
    if not first:
        fresh += state[:live, at] * jnp.exp2((old - top) * scale)
    state[:live, at] = fresh
    state[live : live + 1, at] = top


def fold_all(work):
    ahead = scores(work[0][0], work[0][2]())
    for i, (_, vt, _, state, at) in enumerate(work):
        s = ahead
        if i + 1 < len(work):
            ahead = scores(work[i + 1][0], work[i + 1][2]())
        fold(s, vt, state, at)


def values_and_ones(v, count=None):
    if count is not None:
        row = lax.broadcasted_iota(jnp.int32, v.shape, 0)
        v = jnp.where(row < count, v, jnp.zeros_like(v))
    n = v.shape[0]
    lane = lax.broadcasted_iota(jnp.int32, (SUMS - HEAD_SIZE, n), 1)
    row = lax.broadcasted_iota(jnp.int32, (SUMS - HEAD_SIZE, n), 0)
    live = row < 8
    if count is not None:
        live = live & (lane < count)
    ones = jnp.where(live, 1.0, 0.0).astype(jnp.bfloat16)
    return jnp.concatenate([v.T, ones], axis=0)


def attend_early(place, query, own, sets, after, name):
    rows = query.shape[0]
    kv_local = own.shape[1] // (2 * HEAD_SIZE)
    ratio = query.shape[1] // HEAD_SIZE // kv_local
    wide = ratio * TILE
    count = rows // TILE

    def body(place_ref, q_ref, own_ref, *refs):
        out = refs[-1]
        for g in range(kv_local):
            base = g * 2 * HEAD_SIZE
            k = own_ref[:, base : base + HEAD_SIZE]
            vt = values_and_ones(own_ref[:, base + HEAD_SIZE : base + 2 * HEAD_SIZE])
            for t in range(count):
                upto = (t + 1) * TILE
                column = lax.broadcasted_iota(jnp.int32, (upto, wide), 1) % TILE + t * TILE
                key = lax.broadcasted_iota(jnp.int32, (upto, wide), 0)
                s = jnp.where(key <= column, scores(k[:upto], stacked(q_ref, t, ratio, g)), -1e30)
                fold(s, vt[:, :upto], out.at[g], slice(t * wide, (t + 1) * wide), first=True)
        for i in range(len(sets)):
            k_ref, vt_ref = refs[2 * i], refs[2 * i + 1]
            fold_all(
                [
                    (
                        k_ref[g],
                        vt_ref[g],
                        lambda g=g, t=t: stacked(q_ref, t, ratio, g),
                        out.at[g],
                        slice(t * wide, (t + 1) * wide),
                    )
                    for g in range(kv_local)
                    for t in range(count)
                ]
            )

    def whole(a):
        return pl.BlockSpec(a.shape, lambda i, place: (0,) * len(a.shape))

    args = [query, own, *[a for s in sets for a in s]]
    state_shape = jax.ShapeDtypeStruct((kv_local, SUMS, count * wide), jnp.float32)
    return pl.pallas_call(
        body,
        grid_spec=pltpu.PrefetchScalarGridSpec(
            num_scalar_prefetch=1,
            grid=(1,),
            in_specs=[whole(a) for a in args] + [ANY] * len(after),
            out_specs=whole(state_shape),
        ),
        out_shape=state_shape,
        name=name,
        cost_estimate=SMALL,
        compiler_params=pltpu.CompilerParams(vmem_limit_bytes=VMEM),
    )(place, *args, *after)


def attend_late(place, queries, states, arrived, rows, cache, start, total, last, after):
    kv_width = arrived[0].shape[1]
    kv_local = kv_width // (2 * HEAD_SIZE)
    ratio = queries[0].shape[1] // HEAD_SIZE // kv_local
    wide = ratio * TILE
    n_keys = sum(a.shape[0] for a in arrived)
    most = n_keys - rows
    n = len(queries)
    n_cache = 0 if cache is None else 1

    def body(place_ref, *refs):
        refs = list(refs)
        q_refs = [refs.pop(0) for _ in queries]
        state_refs = [refs.pop(0).at[0] for _ in states]
        arrived_refs = [refs.pop(0) for _ in arrived]
        for _ in range(n_cache + len(after)):
            refs.pop(0)
        cache_ref = refs.pop(0)
        if last:
            out = refs.pop(0)
            k_ref, vt_ref, kv, piece, sems, *work = refs
        else:
            work = [refs.pop(0).at[0] for _ in states]
            k_out, vt_out = refs.pop(0), refs.pop(0)
            k_ref, vt_ref, kv, piece, sems = refs
        g = pl.program_id(0)
        me, length, span = place_ref[0], place_ref[1], place_ref[2]
        count = me * rows

        def prepared(h, keys, count):
            base = h * 2 * HEAD_SIZE
            k = kv[:keys, base : base + HEAD_SIZE]
            row = lax.broadcasted_iota(jnp.int32, k.shape, 0)
            k = jnp.where(row < count, k, jnp.broadcast_to(k[:16][:1], k.shape))
            v = kv[:keys, base + HEAD_SIZE : base + 2 * HEAD_SIZE]
            return k, values_and_ones(v, count)

        def copies():
            return [
                pltpu.make_async_copy(
                    piece.at[j], cache_ref.at[j, pl.ds(start, rows), :], sems.at[j]
                )
                for j in range(GROUPS)
            ]

        @pl.when(g == 0)
        def _():
            def put(stretch, value):
                kv[pl.ds(pl.multiple_of(stretch * rows, 64), rows), :] = value

            if len(arrived) == 1:
                kv[:n_keys, :] = arrived_refs[0][...]
            else:
                half = len(arrived_refs) // 2
                for j, part in enumerate([arrived_refs[:half], arrived_refs[half:]]):
                    found = [
                        ref[i * rows : (i + 1) * rows, :]
                        for ref in part
                        for i in range(ref.shape[0] // rows)
                    ]
                    for i, block in enumerate(found):
                        put(me ^ (2 * i + j), block)
            for j in range(GROUPS):
                value = kv[pl.ds(pl.multiple_of((span + j) * rows, 64), rows), :]
                index = (span + j) * total + start
                index += lax.broadcasted_iota(jnp.int32, value.shape, 0)
                piece[j] = jnp.where(index < length, value, jnp.zeros_like(value))
            for c in copies():
                c.start()
            for h in range(kv_local):
                k_ref[h], vt_ref[h] = prepared(h, most, count)

        for s, w in zip(state_refs, work):
            w[...] = s[...]
        tiles = [
            (
                k_ref.at[g],
                vt_ref.at[g],
                lambda ref=ref, t=t: stacked(ref, t, ratio),
                w,
                slice(t * wide, (t + 1) * wide),
            )
            for ref, w in zip(q_refs, work)
            for t in range(ref.shape[0] // TILE)
        ]

        @pl.when(count > 0)
        def _():
            fold_all([(k[...], vt[...], *rest) for k, vt, *rest in tiles])

        if last:
            for i, (_, _, _, w, at) in enumerate(tiles):
                done = (w[:HEAD_SIZE, at] / w[HEAD_SIZE : HEAD_SIZE + 1, at]).T
                for h in range(ratio):
                    out[i * TILE : (i + 1) * TILE, h * HEAD_SIZE : (h + 1) * HEAD_SIZE] = done[
                        h * TILE : (h + 1) * TILE
                    ].astype(jnp.bfloat16)
        else:
            for h in range(kv_local):

                @pl.when(g == h)
                def _():
                    k_out[0], vt_out[0] = prepared(h, n_keys, count + rows)


        @pl.when(g == kv_local - 1)
        def _():
            for c in copies():
                c.wait()

    def whole(a):
        return pl.BlockSpec(a.shape, lambda g, place: (0,) * len(a.shape))

    def by_group(a):
        return pl.BlockSpec((1,) + a.shape[1:], lambda g, place: (g,) + (0,) * (len(a.shape) - 1))

    k_shape = jax.ShapeDtypeStruct((kv_local, n_keys, HEAD_SIZE), jnp.bfloat16)
    vt_shape = jax.ShapeDtypeStruct((kv_local, SUMS, n_keys), jnp.bfloat16)
    cache_shape = jax.ShapeDtypeStruct((GROUPS, total, kv_width), jnp.bfloat16)
    args = [*queries, *states, *arrived]
    in_specs = [pl.BlockSpec((q.shape[0], ratio * HEAD_SIZE), lambda g, place: (0, g)) for q in queries]
    in_specs += [by_group(s) for s in states] + [whole(a) for a in arrived]
    aliases = {}
    if cache is not None:
        args.append(cache)
        in_specs.append(ANY)
        aliases[len(args)] = 0
    scratch = [
        pltpu.VMEM((kv_local, most, HEAD_SIZE), jnp.bfloat16),
        pltpu.VMEM((kv_local, SUMS, most), jnp.bfloat16),
        pltpu.VMEM((n_keys, kv_width), jnp.bfloat16),
        pltpu.VMEM((GROUPS, rows, kv_width), jnp.bfloat16),
        pltpu.SemaphoreType.DMA((GROUPS,)),
    ]
    if last:
        out_shape = [cache_shape, jax.ShapeDtypeStruct((total, queries[0].shape[1]), jnp.bfloat16)]
        out_specs = [ANY, pl.BlockSpec((total, ratio * HEAD_SIZE), lambda g, place: (0, g))]
        scratch += [pltpu.VMEM(s.shape[1:], jnp.float32) for s in states]
    else:
        out_shape = [cache_shape, *[jax.ShapeDtypeStruct(s.shape, s.dtype) for s in states]]
        out_shape += [k_shape, vt_shape]
        out_specs = [ANY] + [by_group(s) for s in out_shape[1:]]
        for i in range(n):
            aliases[1 + n + i] = 1 + i
    return pl.pallas_call(
        body,
        grid_spec=pltpu.PrefetchScalarGridSpec(
            num_scalar_prefetch=1,
            grid=(kv_local,),
            in_specs=in_specs + [ANY] * len(after),
            out_specs=out_specs,
            scratch_shapes=scratch,
        ),
        out_shape=out_shape,
        input_output_aliases=aliases,
        name=f"late_{start}",
        cost_estimate=SMALL,
        compiler_params=pltpu.CompilerParams(vmem_limit_bytes=VMEM),
    )(place, *args, *after)


def pack(blocks, after, name):
    rows = blocks[0].shape[0]

    def body(*refs):
        for i in range(len(blocks)):
            refs[-1][i * rows : (i + 1) * rows, :] = refs[i][...]

    spec = pl.BlockSpec(memory_space=pltpu.VMEM)
    shape = (rows * len(blocks), blocks[0].shape[1])
    return pl.pallas_call(
        body,
        in_specs=[spec] * len(blocks) + [ANY] * len(after),
        out_specs=spec,
        out_shape=jax.ShapeDtypeStruct(shape, blocks[0].dtype),
        cost_estimate=SMALL,
        name=name,
    )(*blocks, *after)


def exchange(x, after, name, pieces=1):
    even = [x] + [paired(x, "chain", mask) for mask in range(2, lax.axis_size("chain"), 2)]
    size = len(even) // pieces
    even = [
        pack(even[i * size : (i + 1) * size], after, f"{name}_{i}") for i in range(pieces)
    ]
    return (*even, *[paired(e, "chain", 1) for e in even])


def local(tokens, gain, w_query, key_value_weight, offsets, lengths):
    rows = tokens.shape[0]
    kv_local = key_value_weight.shape[1] // (2 * HEAD_SIZE)
    me = lax.axis_index("chain")
    chain = lax.axis_size("chain")
    tp = lax.axis_size("tp")
    lane = lax.axis_index("tp")

    half = HEAD_SIZE // 2
    freq = jnp.power(
        jnp.float32(500000.0), -2.0 * jnp.arange(half).astype(jnp.float32) / HEAD_SIZE
    )
    position = offsets[0] + jnp.arange(rows, dtype=jnp.int32)
    angle = position.astype(jnp.float32)[:, None] * freq[None, :]
    cosine, sine = jnp.cos(angle), jnp.sin(angle)
    cosine = jnp.concatenate([cosine, cosine], axis=1)
    sine = jnp.concatenate([-sine, sine], axis=1)

    members = chain // GROUPS
    span = me % members * GROUPS
    length = jnp.sum(jnp.where(jnp.arange(GROUPS) == me // members, lengths, 0))
    place = jnp.stack([me, length, span]).astype(jnp.int32)

    sizes = [rows * FIRST // 8, rows * (8 - FIRST) // 8]
    starts = [0, sizes[0]]
    weights = (w_query, key_value_weight)
    arrived = [None] * len(sizes)

    def send(r, after):
        chunk = cut(tokens, starts[r], sizes[r], after, f"cut_{r}")
        if tp == 4:
            arrived[r] = [chunk, shifted(chunk, "tp", 1), shifted(chunk, "tp", -1)]
        else:
            arrived[r] = [lax.all_gather(chunk, "tp", axis=0)]
        return chunk

    def forward(r, i, after):
        if tp != 4:
            return arrived[r][0]
        half = sizes[r] // 2
        part = cut(arrived[r][i], (i - 1) * half, half, after, f"pass_{r}_{i}")
        arrived[r].append(shifted(part, "tp", 3 - 2 * i))
        return part

    def near(r, after):
        if tp == 4:
            parts, which, carry = arrived[r][1:3], order[1:3], (own, starts[r])
        else:
            parts, which, carry = [arrived[r][0][i] for i in range(tp - 1)], order[:-1], None
        return add_products(parts, which, gain, weights, carry, 1024, after, f"near_{r}")

    def finish(r, weight, turned, sums, squares, after, name):
        part = arrived[r][3:] if tp == 4 else [arrived[r][0][tp - 1]]
        at = slice(starts[r], starts[r] + sizes[r])
        tables = (cosine[at], sine[at])
        return finish_products(
            part, order[-1:], gain, weight, turned, sums, squares, tables, after, f"{name}_{r}"
        )

    def keys_and_queries(r, sums, after=()):
        q_sums, kv_sums, squares = sums
        kv = finish(r, key_value_weight, (True, False), kv_sums, squares, after, "kv")
        query = finish(r, w_query, (True, True), q_sums, squares, (kv,), "query")
        return kv, query

    if tp == 4:
        order = jnp.stack([lane, (lane + 3) % 4, (lane + 1) % 4, (lane + 2) % 4])
        order = order.astype(jnp.int32)
    else:
        order = jnp.arange(tp, dtype=jnp.int32)

    step = send(0, ())
    if tp == 4:
        own = add_products([tokens], order[:1], gain, weights, None, 1024, (step,), "own")
        step = own[-1]
    step = forward(0, 1, (step,))
    step = forward(0, 2, (step,))
    sums = near(0, (step,))
    step = send(1, (sums[2],))
    kv_0, query_0 = keys_and_queries(0, sums, (step,))
    keys = exchange(kv_0, (query_0,), "pack_0", 2)
    state_0 = attend_early(place, query_0, kv_0, [], keys[:1], "early_0")
    step = forward(1, 1, (state_0,))
    cache, state_0, k, vt = attend_late(
        place, [query_0], [state_0], keys, sizes[0], None, 0, rows, False, (step,)
    )
    step = forward(1, 2, (k,))
    sums = near(1, (step,))
    kv_1, query_1 = keys_and_queries(1, sums)
    keys = exchange(kv_1, (query_1,), "pack_1")
    state_1 = attend_early(place, query_1, kv_1, [(k, vt)], keys[:1], "early_1")
    queries, states = [query_0, query_1], [state_0, state_1]
    cache, context = attend_late(
        place, queries, states, keys, sizes[1], cache, starts[1], rows, True, ()
    )
    return context, cache.reshape(GROUPS * rows, key_value_weight.shape[1])


def solution(mesh):
    in_specs = (P("chain", "tp"), P(), P(None, "tp"), P(None, "tp"), P("chain"), P())
    out_specs = (P("chain", "tp"), P("chain", "tp"))
    return jax.shard_map(local, mesh=mesh, in_specs=in_specs, out_specs=out_specs, check_vma=False)
```

```python
import math

import jax
import jax.numpy as jnp
from jax import lax
from jax.experimental import pallas as pl
from jax.experimental.pallas import tpu as pltpu
from jax.sharding import PartitionSpec as P

HEAD_SIZE = 128
GROUPS = 4
TILE = 64
FIRST = 4
SUMS = HEAD_SIZE + 16
VMEM = 63 * 1024 * 1024
SMALL = pl.CostEstimate(flops=1000, bytes_accessed=1000, transcendentals=0)
ANY = pl.BlockSpec(memory_space=pl.ANY)


def shifted(x, axis, by):
    n = lax.axis_size(axis)
    return lax.ppermute(x, axis, [(i, (i + by) % n) for i in range(n)])


def paired(x, axis, mask):
    return lax.ppermute(x, axis, [(i, i ^ mask) for i in range(lax.axis_size(axis))])


def cut(x, start, rows, after, name):
    def body(x_ref, *refs):
        out, held, sems = refs[-3:]
        for i, (a, b) in enumerate([(x_ref.at[pl.ds(start, rows), :], held), (held, out)]):
            copy = pltpu.make_async_copy(a, b, sems.at[i])
            copy.start()
            copy.wait()

    return pl.pallas_call(
        body,
        in_specs=[pl.BlockSpec(memory_space=pltpu.HBM)] + [ANY] * len(after),
        out_specs=pl.BlockSpec(memory_space=pltpu.HBM),
        out_shape=jax.ShapeDtypeStruct((rows, x.shape[1]), x.dtype),
        scratch_shapes=[
            pltpu.VMEM((rows, x.shape[1]), x.dtype),
            pltpu.SemaphoreType.DMA((2,)),
        ],
        cost_estimate=SMALL,
        name=name,
    )(x, *after)


def normed_rows(parts_refs, gain_ref, x_ref, square_ref):
    at = 0
    for ref in parts_refs:
        rows = slice(at, at + ref.shape[0])
        x = ref[...].astype(jnp.float32)
        x_ref[rows, :] = (x * gain_ref[0]).astype(jnp.bfloat16)
        square = x * x
        square_ref[rows, :] += sum(square[:, i : i + 128] for i in range(0, x.shape[1], 128))
        at += ref.shape[0]


def add_products(parts, order, gain, weights, carry, depth, after, name):
    count = len(parts)
    rows, width = parts[0].shape
    pieces = rows // TILE
    depth = min(depth, width)
    steps = width // depth
    model = weights[0].shape[0]
    n = len(weights)

    def body(order_ref, *refs):
        refs = list(refs)
        part_refs = [refs.pop(0) for _ in parts]
        gain_ref = refs.pop(0)
        w_refs = [refs.pop(0) for _ in weights]
        carry_refs = [[refs.pop(0) for _ in range(pieces)] for _ in range(n + 1)] if carry else None
        *sums, x_ref = refs[len(after) :]
        step = pl.program_id(0)

        @pl.when(step == 0)
        def _():
            for i, s in enumerate(sums):
                if carry:
                    for piece, ref in enumerate(carry_refs[i]):
                        s[piece * TILE : (piece + 1) * TILE, :] = ref[...]
                else:
                    s[...] = jnp.zeros_like(s)

        for i in range(count):

            @pl.when(step // steps == i)
            def _():
                normed_rows([part_refs[i]], gain_ref, x_ref, sums[-1])

        for s, w in zip(sums, w_refs):
            s[...] += jnp.dot(x_ref[...], w[...], preferred_element_type=jnp.float32)

    def part_spec(i):
        return pl.BlockSpec(
            (rows, depth), lambda s, order: (0, jnp.clip(s - i * steps, 0, steps - 1))
        )

    def carry_spec(columns, piece):
        return pl.BlockSpec((TILE, columns), lambda s, order: (carry[1] // TILE + piece, 0))

    def block(s, order):
        return order[s // steps] * steps + s % steps

    columns = [w.shape[1] for w in weights]
    out_shape = [jax.ShapeDtypeStruct((rows, c), jnp.float32) for c in (*columns, 128)]
    in_specs = [part_spec(i) for i in range(count)]
    in_specs += [pl.BlockSpec((1, 1, depth), lambda s, order: (block(s, order), 0, 0))]
    in_specs += [
        pl.BlockSpec((depth, c), lambda s, order: (block(s, order), 0)) for c in columns
    ]
    if carry:
        in_specs += [carry_spec(s.shape[1], p) for s in out_shape for p in range(pieces)]
    return pl.pallas_call(
        body,
        grid_spec=pltpu.PrefetchScalarGridSpec(
            num_scalar_prefetch=1,
            grid=(count * steps,),
            in_specs=in_specs + [ANY] * len(after),
            out_specs=[pl.BlockSpec(s.shape, lambda s, order: (0, 0)) for s in out_shape],
            scratch_shapes=[pltpu.VMEM((rows, depth), jnp.bfloat16)],
        ),
        out_shape=out_shape,
        name=name,
        cost_estimate=SMALL,
        compiler_params=pltpu.CompilerParams(vmem_limit_bytes=VMEM),
    )(
        order,
        *parts,
        gain.reshape(model // depth, 1, depth),
        *weights,
        *([a for a in carry[0] for _ in range(pieces)] if carry else ()),
        *after,
    )


def finish_products(part, order, gain, weight, turned, sums, squares, tables, after, name):
    width = part[0].shape[1]
    rows = sum(p.shape[0] for p in part)
    model, columns = weight.shape
    wide = min(columns, 512)

    def body(order_ref, *refs):
        refs = list(refs)
        part_refs = [refs.pop(0) for _ in part]
        gain_ref, w_ref, sums_ref, squares_ref, cosine_ref, sine_ref = refs[:6]
        out, x_ref, square_ref = refs[-3:]

        @pl.when(pl.program_id(0) == 0)
        def _():
            square_ref[...] = squares_ref[...]
            normed_rows(part_refs, gain_ref, x_ref, square_ref)
            total = jnp.sum(square_ref[...], axis=1, keepdims=True)
            square_ref[...] = jnp.broadcast_to(lax.rsqrt(total / model + 1e-05), square_ref.shape)

        inv = square_ref[...]
        sums = sums_ref[...] + jnp.dot(x_ref[...], w_ref[...], preferred_element_type=jnp.float32)
        for i, at in enumerate(range(0, wide, 128)):
            u = sums[:, at : at + 128] * inv
            if turned[i % 2]:
                u = u * cosine_ref[...] + pltpu.roll(u, 64, 1) * sine_ref[...]
            out[:, at : at + 128] = u.astype(jnp.bfloat16)

    def whole(a):
        return pl.BlockSpec(a.shape, lambda s, order: (0, 0))

    by_columns = pl.BlockSpec((rows, wide), lambda s, order: (0, s))
    return pl.pallas_call(
        body,
        grid_spec=pltpu.PrefetchScalarGridSpec(
            num_scalar_prefetch=1,
            grid=(columns // wide,),
            in_specs=[whole(p) for p in part]
            + [pl.BlockSpec((1, 1, width), lambda s, order: (order[0], 0, 0))]
            + [pl.BlockSpec((width, wide), lambda s, order: (order[0], s))]
            + [by_columns, whole(squares), whole(tables[0]), whole(tables[1])]
            + [ANY] * len(after),
            out_specs=by_columns,
            scratch_shapes=[
                pltpu.VMEM((rows, width), jnp.bfloat16),
                pltpu.VMEM((rows, 128), jnp.float32),
            ],
        ),
        out_shape=jax.ShapeDtypeStruct((rows, columns), jnp.bfloat16),
        name=name,
        cost_estimate=SMALL,
        compiler_params=pltpu.CompilerParams(vmem_limit_bytes=VMEM),
    )(order, *part, gain.reshape(model // width, 1, width), weight, sums, squares, *tables, *after)


def stacked(q_ref, tile, ratio, group=0):
    rows = slice(tile * TILE, (tile + 1) * TILE)
    heads = range(group * ratio, (group + 1) * ratio)
    return jnp.concatenate(
        [q_ref[rows, h * HEAD_SIZE : (h + 1) * HEAD_SIZE] for h in heads], axis=0
    )


def scores(k, q):
    return lax.dot_general(k, q, (((1,), (1,)), ((), ())), preferred_element_type=jnp.float32)


def fold(s, vt, state, at, first=False):
    scale = math.log2(math.e) / math.sqrt(HEAD_SIZE)
    live = HEAD_SIZE + 8
    top = jnp.max(s, axis=0, keepdims=True)
    if not first:
        old = state[live : live + 1, at]
        top = jnp.maximum(old, top)
    p = jnp.exp2((s - top) * scale).astype(jnp.bfloat16)
    fresh = jnp.dot(vt, p, preferred_element_type=jnp.float32)[:live]
    if not first:
        fresh += state[:live, at] * jnp.exp2((old - top) * scale)
    state[:live, at] = fresh
    state[live : live + 1, at] = top


def fold_all(work):
    ahead = scores(work[0][0], work[0][2]())
    for i, (_, vt, _, state, at) in enumerate(work):
        s = ahead
        if i + 1 < len(work):
            ahead = scores(work[i + 1][0], work[i + 1][2]())
        fold(s, vt, state, at)


def by_stretches(take, count, most, enough, rows):
    @pl.when(count >= enough)
    def _():
        take(pl.ds(0, most * rows))

    @pl.when(count < enough)
    def _():
        def two(i, _):
            take(pl.ds(pl.multiple_of(i * 2 * rows, 128), 2 * rows))
            return 0

        lax.fori_loop(0, (count + 1) // 2, two, 0)


def values_and_ones(v, count=None):
    if count is not None:
        row = lax.broadcasted_iota(jnp.int32, v.shape, 0)
        v = jnp.where(row < count, v, jnp.zeros_like(v))
    n = v.shape[0]
    lane = lax.broadcasted_iota(jnp.int32, (SUMS - HEAD_SIZE, n), 1)
    row = lax.broadcasted_iota(jnp.int32, (SUMS - HEAD_SIZE, n), 0)
    live = row < 8
    if count is not None:
        live = live & (lane < count)
    ones = jnp.where(live, 1.0, 0.0).astype(jnp.bfloat16)
    return jnp.concatenate([v.T, ones], axis=0)


def attend_early(place, query, own, sets, after, name):
    rows = query.shape[0]
    kv_local = own.shape[1] // (2 * HEAD_SIZE)
    ratio = query.shape[1] // HEAD_SIZE // kv_local
    wide = ratio * TILE
    count = rows // TILE
    chain = lax.axis_size("chain")

    def body(place_ref, q_ref, own_ref, *refs):
        out = refs[-1]
        for g in range(kv_local):
            base = g * 2 * HEAD_SIZE
            k = own_ref[:, base : base + HEAD_SIZE]
            vt = values_and_ones(own_ref[:, base + HEAD_SIZE : base + 2 * HEAD_SIZE])
            for t in range(count):
                upto = (t + 1) * TILE
                column = lax.broadcasted_iota(jnp.int32, (upto, wide), 1) % TILE + t * TILE
                key = lax.broadcasted_iota(jnp.int32, (upto, wide), 0)
                s = jnp.where(key <= column, scores(k[:upto], stacked(q_ref, t, ratio, g)), -1e30)
                fold(s, vt[:, :upto], out.at[g], slice(t * wide, (t + 1) * wide), first=True)
        for i, (set_keys, _) in enumerate(sets):
            k_ref, vt_ref = refs[2 * i], refs[2 * i + 1]

            def take(at, k_ref=k_ref, vt_ref=vt_ref):
                fold_all(
                    [
                        (
                            k_ref[g, at, :],
                            vt_ref[g, :, at],
                            lambda g=g, t=t: stacked(q_ref, t, ratio, g),
                            out.at[g],
                            slice(t * wide, (t + 1) * wide),
                        )
                        for g in range(kv_local)
                        for t in range(count)
                    ]
                )

            by_stretches(take, place_ref[0] + 1, chain, chain - 1, set_keys.shape[1] // chain)

    def whole(a):
        return pl.BlockSpec(a.shape, lambda i, place: (0,) * len(a.shape))

    args = [query, own, *[a for s in sets for a in s]]
    state_shape = jax.ShapeDtypeStruct((kv_local, SUMS, count * wide), jnp.float32)
    return pl.pallas_call(
        body,
        grid_spec=pltpu.PrefetchScalarGridSpec(
            num_scalar_prefetch=1,
            grid=(1,),
            in_specs=[whole(a) for a in args] + [ANY] * len(after),
            out_specs=whole(state_shape),
        ),
        out_shape=state_shape,
        name=name,
        cost_estimate=SMALL,
        compiler_params=pltpu.CompilerParams(vmem_limit_bytes=VMEM),
    )(place, *args, *after)


def attend_late(place, queries, states, arrived, rows, cache, start, total, last, after):
    kv_width = arrived[0].shape[1]
    kv_local = kv_width // (2 * HEAD_SIZE)
    ratio = queries[0].shape[1] // HEAD_SIZE // kv_local
    wide = ratio * TILE
    n_keys = sum(a.shape[0] for a in arrived)
    most = n_keys - rows
    n = len(queries)
    n_cache = 0 if cache is None else 1

    def body(place_ref, *refs):
        refs = list(refs)
        q_refs = [refs.pop(0) for _ in queries]
        state_refs = [refs.pop(0).at[0] for _ in states]
        arrived_refs = [refs.pop(0) for _ in arrived]
        for _ in range(n_cache + len(after)):
            refs.pop(0)
        cache_ref = refs.pop(0)
        if last:
            out = refs.pop(0)
            k_ref, vt_ref, kv, piece, sems, *work = refs
        else:
            work = [refs.pop(0).at[0] for _ in states]
            k_out, vt_out = refs.pop(0), refs.pop(0)
            k_ref, vt_ref, kv, piece, sems = refs
        g = pl.program_id(0)
        me, length, span = place_ref[0], place_ref[1], place_ref[2]
        count = me * rows

        def prepared(h, keys, count):
            base = h * 2 * HEAD_SIZE
            k = kv[:keys, base : base + HEAD_SIZE]
            row = lax.broadcasted_iota(jnp.int32, k.shape, 0)
            k = jnp.where(row < count, k, jnp.broadcast_to(k[:16][:1], k.shape))
            v = kv[:keys, base + HEAD_SIZE : base + 2 * HEAD_SIZE]
            return k, values_and_ones(v, count)

        def copies():
            return [
                pltpu.make_async_copy(
                    piece.at[j], cache_ref.at[j, pl.ds(start, rows), :], sems.at[j]
                )
                for j in range(GROUPS)
            ]

        @pl.when(g == 0)
        def _():
            def put(stretch, value):
                kv[pl.ds(pl.multiple_of(stretch * rows, 64), rows), :] = value

            if len(arrived) == 1:
                kv[:n_keys, :] = arrived_refs[0][...]
            else:
                half = len(arrived_refs) // 2
                for j, part in enumerate([arrived_refs[:half], arrived_refs[half:]]):
                    found = [
                        ref[i * rows : (i + 1) * rows, :]
                        for ref in part
                        for i in range(ref.shape[0] // rows)
                    ]
                    for i, block in enumerate(found):
                        put(me ^ (2 * i + j), block)
            for j in range(GROUPS):
                value = kv[pl.ds(pl.multiple_of((span + j) * rows, 64), rows), :]
                index = (span + j) * total + start
                index += lax.broadcasted_iota(jnp.int32, value.shape, 0)
                piece[j] = jnp.where(index < length, value, jnp.zeros_like(value))
            for c in copies():
                c.start()
            for h in range(kv_local):
                k_ref[h], vt_ref[h] = prepared(h, most, count)

        for s, w in zip(state_refs, work):
            w[...] = s[...]
        tiles = [
            (lambda ref=ref, t=t: stacked(ref, t, ratio), w, slice(t * wide, (t + 1) * wide))
            for ref, w in zip(q_refs, work)
            for t in range(ref.shape[0] // TILE)
        ]

        def take(at):
            k, vt = k_ref[g, at, :], vt_ref[g, :, at]
            fold_all([(k, vt, *tile) for tile in tiles])

        by_stretches(take, me, most // rows, most // rows, rows)
        if last:
            for i, (_, w, at) in enumerate(tiles):
                done = (w[:HEAD_SIZE, at] / w[HEAD_SIZE : HEAD_SIZE + 1, at]).T
                for h in range(ratio):
                    out[i * TILE : (i + 1) * TILE, h * HEAD_SIZE : (h + 1) * HEAD_SIZE] = done[
                        h * TILE : (h + 1) * TILE
                    ].astype(jnp.bfloat16)
        else:
            for h in range(kv_local):

                @pl.when(g == h)
                def _():
                    k_out[0], vt_out[0] = prepared(h, n_keys, count + rows)


        @pl.when(g == kv_local - 1)
        def _():
            for c in copies():
                c.wait()

    def whole(a):
        return pl.BlockSpec(a.shape, lambda g, place: (0,) * len(a.shape))

    def by_group(a):
        return pl.BlockSpec((1,) + a.shape[1:], lambda g, place: (g,) + (0,) * (len(a.shape) - 1))

    k_shape = jax.ShapeDtypeStruct((kv_local, n_keys, HEAD_SIZE), jnp.bfloat16)
    vt_shape = jax.ShapeDtypeStruct((kv_local, SUMS, n_keys), jnp.bfloat16)
    cache_shape = jax.ShapeDtypeStruct((GROUPS, total, kv_width), jnp.bfloat16)
    args = [*queries, *states, *arrived]
    in_specs = [pl.BlockSpec((q.shape[0], ratio * HEAD_SIZE), lambda g, place: (0, g)) for q in queries]
    in_specs += [by_group(s) for s in states] + [whole(a) for a in arrived]
    aliases = {}
    if cache is not None:
        args.append(cache)
        in_specs.append(ANY)
        aliases[len(args)] = 0
    scratch = [
        pltpu.VMEM((kv_local, most, HEAD_SIZE), jnp.bfloat16),
        pltpu.VMEM((kv_local, SUMS, most), jnp.bfloat16),
        pltpu.VMEM((n_keys, kv_width), jnp.bfloat16),
        pltpu.VMEM((GROUPS, rows, kv_width), jnp.bfloat16),
        pltpu.SemaphoreType.DMA((GROUPS,)),
    ]
    if last:
        out_shape = [cache_shape, jax.ShapeDtypeStruct((total, queries[0].shape[1]), jnp.bfloat16)]
        out_specs = [ANY, pl.BlockSpec((total, ratio * HEAD_SIZE), lambda g, place: (0, g))]
        scratch += [pltpu.VMEM(s.shape[1:], jnp.float32) for s in states]
    else:
        out_shape = [cache_shape, *[jax.ShapeDtypeStruct(s.shape, s.dtype) for s in states]]
        out_shape += [k_shape, vt_shape]
        out_specs = [ANY] + [by_group(s) for s in out_shape[1:]]
        for i in range(n):
            aliases[1 + n + i] = 1 + i
    return pl.pallas_call(
        body,
        grid_spec=pltpu.PrefetchScalarGridSpec(
            num_scalar_prefetch=1,
            grid=(kv_local,),
            in_specs=in_specs + [ANY] * len(after),
            out_specs=out_specs,
            scratch_shapes=scratch,
        ),
        out_shape=out_shape,
        input_output_aliases=aliases,
        name=f"late_{start}",
        cost_estimate=SMALL,
        compiler_params=pltpu.CompilerParams(vmem_limit_bytes=VMEM),
    )(place, *args, *after)


def pack(blocks, after, name):
    rows = blocks[0].shape[0]

    def body(*refs):
        for i in range(len(blocks)):
            refs[-1][i * rows : (i + 1) * rows, :] = refs[i][...]

    spec = pl.BlockSpec(memory_space=pltpu.VMEM)
    shape = (rows * len(blocks), blocks[0].shape[1])
    return pl.pallas_call(
        body,
        in_specs=[spec] * len(blocks) + [ANY] * len(after),
        out_specs=spec,
        out_shape=jax.ShapeDtypeStruct(shape, blocks[0].dtype),
        cost_estimate=SMALL,
        name=name,
    )(*blocks, *after)


def exchange(x, after, name, pieces=1):
    even = [x] + [paired(x, "chain", mask) for mask in range(2, lax.axis_size("chain"), 2)]
    size = len(even) // pieces
    even = [
        pack(even[i * size : (i + 1) * size], after, f"{name}_{i}") for i in range(pieces)
    ]
    return (*even, *[paired(e, "chain", 1) for e in even])


def local(tokens, gain, w_query, key_value_weight, offsets, lengths):
    rows = tokens.shape[0]
    kv_local = key_value_weight.shape[1] // (2 * HEAD_SIZE)
    me = lax.axis_index("chain")
    chain = lax.axis_size("chain")
    tp = lax.axis_size("tp")
    lane = lax.axis_index("tp")

    half = HEAD_SIZE // 2
    freq = jnp.power(
        jnp.float32(500000.0), -2.0 * jnp.arange(half).astype(jnp.float32) / HEAD_SIZE
    )
    position = offsets[0] + jnp.arange(rows, dtype=jnp.int32)
    angle = position.astype(jnp.float32)[:, None] * freq[None, :]
    cosine, sine = jnp.cos(angle), jnp.sin(angle)
    cosine = jnp.concatenate([cosine, cosine], axis=1)
    sine = jnp.concatenate([-sine, sine], axis=1)

    members = chain // GROUPS
    span = me % members * GROUPS
    length = jnp.sum(jnp.where(jnp.arange(GROUPS) == me // members, lengths, 0))
    place = jnp.stack([me, length, span]).astype(jnp.int32)

    sizes = [rows * FIRST // 8, rows * (8 - FIRST) // 8]
    starts = [0, sizes[0]]
    weights = (w_query, key_value_weight)
    arrived = [None] * len(sizes)

    def send(r, after):
        chunk = cut(tokens, starts[r], sizes[r], after, f"cut_{r}")
        if tp == 4:
            arrived[r] = [chunk, shifted(chunk, "tp", 1), shifted(chunk, "tp", -1)]
        else:
            arrived[r] = [lax.all_gather(chunk, "tp", axis=0)]
        return chunk

    def forward(r, i, after):
        if tp != 4:
            return arrived[r][0]
        half = sizes[r] // 2
        part = cut(arrived[r][i], (i - 1) * half, half, after, f"pass_{r}_{i}")
        arrived[r].append(shifted(part, "tp", 3 - 2 * i))
        return part

    def near(r, after):
        if tp == 4:
            parts, which, carry = arrived[r][1:3], order[1:3], (own, starts[r])
        else:
            parts, which, carry = [arrived[r][0][i] for i in range(tp - 1)], order[:-1], None
        return add_products(parts, which, gain, weights, carry, 1024, after, f"near_{r}")

    def finish(r, weight, turned, sums, squares, after, name):
        part = arrived[r][3:] if tp == 4 else [arrived[r][0][tp - 1]]
        at = slice(starts[r], starts[r] + sizes[r])
        tables = (cosine[at], sine[at])
        return finish_products(
            part, order[-1:], gain, weight, turned, sums, squares, tables, after, f"{name}_{r}"
        )

    def keys_and_queries(r, sums, after=()):
        q_sums, kv_sums, squares = sums
        kv = finish(r, key_value_weight, (True, False), kv_sums, squares, after, "kv")
        query = finish(r, w_query, (True, True), q_sums, squares, (kv,), "query")
        return kv, query

    if tp == 4:
        order = jnp.stack([lane, (lane + 3) % 4, (lane + 1) % 4, (lane + 2) % 4])
        order = order.astype(jnp.int32)
    else:
        order = jnp.arange(tp, dtype=jnp.int32)

    step = send(0, ())
    if tp == 4:
        own = add_products([tokens], order[:1], gain, weights, None, 1024, (step,), "own")
        step = own[-1]
    step = forward(0, 1, (step,))
    step = forward(0, 2, (step,))
    sums = near(0, (step,))
    step = send(1, (sums[2],))
    kv_0, query_0 = keys_and_queries(0, sums, (step,))
    keys = exchange(kv_0, (query_0,), "pack_0", 2)
    state_0 = attend_early(place, query_0, kv_0, [], keys[:1], "early_0")
    step = forward(1, 1, (state_0,))
    cache, state_0, k, vt = attend_late(
        place, [query_0], [state_0], keys, sizes[0], None, 0, rows, False, (step,)
    )
    step = forward(1, 2, (k,))
    sums = near(1, (step,))
    kv_1, query_1 = keys_and_queries(1, sums)
    keys = exchange(kv_1, (query_1,), "pack_1")
    state_1 = attend_early(place, query_1, kv_1, [(k, vt)], keys[:1], "early_1")
    queries, states = [query_0, query_1], [state_0, state_1]
    cache, context = attend_late(
        place, queries, states, keys, sizes[1], cache, starts[1], rows, True, ()
    )
    return context, cache.reshape(GROUPS * rows, key_value_weight.shape[1])


def solution(mesh):
    in_specs = (P("chain", "tp"), P(), P(None, "tp"), P(None, "tp"), P("chain"), P())
    out_specs = (P("chain", "tp"), P("chain", "tp"))
    return jax.shard_map(local, mesh=mesh, in_specs=in_specs, out_specs=out_specs, check_vma=False)
```

```python
import math

import jax
import jax.numpy as jnp
from jax import lax
from jax.experimental import pallas as pl
from jax.experimental.pallas import tpu as pltpu
from jax.sharding import PartitionSpec as P

HEAD_SIZE = 128
GROUPS = 4
TILE = 64
FIRST = 4
SUMS = HEAD_SIZE + 16
VMEM = 63 * 1024 * 1024
SMALL = pl.CostEstimate(flops=1000, bytes_accessed=1000, transcendentals=0)
ANY = pl.BlockSpec(memory_space=pl.ANY)


def shifted(x, axis, by):
    n = lax.axis_size(axis)
    return lax.ppermute(x, axis, [(i, (i + by) % n) for i in range(n)])


def paired(x, axis, mask):
    return lax.ppermute(x, axis, [(i, i ^ mask) for i in range(lax.axis_size(axis))])


def cut(x, start, rows, after, name):
    def body(x_ref, *refs):
        out, held, sems = refs[-3:]
        for i, (a, b) in enumerate([(x_ref.at[pl.ds(start, rows), :], held), (held, out)]):
            copy = pltpu.make_async_copy(a, b, sems.at[i])
            copy.start()
            copy.wait()

    return pl.pallas_call(
        body,
        in_specs=[pl.BlockSpec(memory_space=pltpu.HBM)] + [ANY] * len(after),
        out_specs=pl.BlockSpec(memory_space=pltpu.HBM),
        out_shape=jax.ShapeDtypeStruct((rows, x.shape[1]), x.dtype),
        scratch_shapes=[
            pltpu.VMEM((rows, x.shape[1]), x.dtype),
            pltpu.SemaphoreType.DMA((2,)),
        ],
        cost_estimate=SMALL,
        name=name,
    )(x, *after)


def normed_rows(parts_refs, gain_ref, x_ref, square_ref):
    at = 0
    for ref in parts_refs:
        rows = slice(at, at + ref.shape[0])
        x = ref[...].astype(jnp.float32)
        x_ref[rows, :] = (x * gain_ref[0]).astype(jnp.bfloat16)
        square = x * x
        square_ref[rows, :] += sum(square[:, i : i + 128] for i in range(0, x.shape[1], 128))
        at += ref.shape[0]


def add_products(parts, order, gain, weights, carry, depth, after, name):
    count = len(parts)
    rows, width = parts[0].shape
    pieces = rows // TILE
    depth = min(depth, width)
    steps = width // depth
    model = weights[0].shape[0]
    n = len(weights)

    def body(order_ref, *refs):
        refs = list(refs)
        part_refs = [refs.pop(0) for _ in parts]
        gain_ref = refs.pop(0)
        w_refs = [refs.pop(0) for _ in weights]
        carry_refs = [[refs.pop(0) for _ in range(pieces)] for _ in range(n + 1)] if carry else None
        *sums, x_ref = refs[len(after) :]
        step = pl.program_id(0)

        @pl.when(step == 0)
        def _():
            for i, s in enumerate(sums):
                if carry:
                    for piece, ref in enumerate(carry_refs[i]):
                        s[piece * TILE : (piece + 1) * TILE, :] = ref[...]
                else:
                    s[...] = jnp.zeros_like(s)

        for i in range(count):

            @pl.when(step // steps == i)
            def _():
                normed_rows([part_refs[i]], gain_ref, x_ref, sums[-1])

        for s, w in zip(sums, w_refs):
            wide = w.shape[1] if carry else math.gcd(w.shape[1], 512)

            def add(i, _, s=s, w=w, wide=wide):
                at = pl.ds(pl.multiple_of(i * wide, 128), wide)
                s[:, at] += jnp.dot(x_ref[...], w[:, at], preferred_element_type=jnp.float32)
                return 0

            lax.fori_loop(0, w.shape[1] // wide, add, 0)

    def part_spec(i):
        return pl.BlockSpec(
            (rows, depth), lambda s, order: (0, jnp.clip(s - i * steps, 0, steps - 1))
        )

    def carry_spec(columns, piece):
        return pl.BlockSpec((TILE, columns), lambda s, order: (carry[1] // TILE + piece, 0))

    def block(s, order):
        return order[s // steps] * steps + s % steps

    columns = [w.shape[1] for w in weights]
    out_shape = [jax.ShapeDtypeStruct((rows, c), jnp.float32) for c in (*columns, 128)]
    in_specs = [part_spec(i) for i in range(count)]
    in_specs += [pl.BlockSpec((1, 1, depth), lambda s, order: (block(s, order), 0, 0))]
    in_specs += [
        pl.BlockSpec((depth, c), lambda s, order: (block(s, order), 0)) for c in columns
    ]
    if carry:
        in_specs += [carry_spec(s.shape[1], p) for s in out_shape for p in range(pieces)]
    return pl.pallas_call(
        body,
        grid_spec=pltpu.PrefetchScalarGridSpec(
            num_scalar_prefetch=1,
            grid=(count * steps,),
            in_specs=in_specs + [ANY] * len(after),
            out_specs=[pl.BlockSpec(s.shape, lambda s, order: (0, 0)) for s in out_shape],
            scratch_shapes=[pltpu.VMEM((rows, depth), jnp.bfloat16)],
        ),
        out_shape=out_shape,
        name=name,
        cost_estimate=SMALL,
        compiler_params=pltpu.CompilerParams(vmem_limit_bytes=VMEM),
    )(
        order,
        *parts,
        gain.reshape(model // depth, 1, depth),
        *weights,
        *([a for a in carry[0] for _ in range(pieces)] if carry else ()),
        *after,
    )


def finish_products(part, order, gain, weight, turned, sums, squares, tables, after, name):
    width = part[0].shape[1]
    rows = sum(p.shape[0] for p in part)
    model, columns = weight.shape
    wide = min(columns, 1024)

    def body(order_ref, *refs):
        refs = list(refs)
        part_refs = [refs.pop(0) for _ in part]
        gain_ref, w_ref, sums_ref, squares_ref, cosine_ref, sine_ref = refs[:6]
        out, x_ref, square_ref = refs[-3:]

        @pl.when(pl.program_id(0) == 0)
        def _():
            square_ref[...] = squares_ref[...]
            normed_rows(part_refs, gain_ref, x_ref, square_ref)
            total = jnp.sum(square_ref[...], axis=1, keepdims=True)
            square_ref[...] = jnp.broadcast_to(lax.rsqrt(total / model + 1e-05), square_ref.shape)

        inv = square_ref[...]
        sums = sums_ref[...] + jnp.dot(x_ref[...], w_ref[...], preferred_element_type=jnp.float32)
        for i, at in enumerate(range(0, wide, 128)):
            u = sums[:, at : at + 128] * inv
            if turned[i % 2]:
                u = u * cosine_ref[...] + pltpu.roll(u, 64, 1) * sine_ref[...]
            out[:, at : at + 128] = u.astype(jnp.bfloat16)

    def whole(a):
        return pl.BlockSpec(a.shape, lambda s, order: (0, 0))

    by_columns = pl.BlockSpec((rows, wide), lambda s, order: (0, s))
    return pl.pallas_call(
        body,
        grid_spec=pltpu.PrefetchScalarGridSpec(
            num_scalar_prefetch=1,
            grid=(columns // wide,),
            in_specs=[whole(p) for p in part]
            + [pl.BlockSpec((1, 1, width), lambda s, order: (order[0], 0, 0))]
            + [pl.BlockSpec((width, wide), lambda s, order: (order[0], s))]
            + [by_columns, whole(squares), whole(tables[0]), whole(tables[1])]
            + [ANY] * len(after),
            out_specs=by_columns,
            scratch_shapes=[
                pltpu.VMEM((rows, width), jnp.bfloat16),
                pltpu.VMEM((rows, 128), jnp.float32),
            ],
        ),
        out_shape=jax.ShapeDtypeStruct((rows, columns), jnp.bfloat16),
        name=name,
        cost_estimate=SMALL,
        compiler_params=pltpu.CompilerParams(vmem_limit_bytes=VMEM),
    )(order, *part, gain.reshape(model // width, 1, width), weight, sums, squares, *tables, *after)


def stacked(q_ref, tile, ratio, group=0):
    rows = pl.ds(pl.multiple_of(tile * TILE, TILE), TILE)
    return jnp.concatenate(
        [
            q_ref[rows, pl.ds(pl.multiple_of((group * ratio + h) * HEAD_SIZE, HEAD_SIZE), HEAD_SIZE)]
            for h in range(ratio)
        ],
        axis=0,
    )


def scores(k, q):
    return lax.dot_general(k, q, (((1,), (1,)), ((), ())), preferred_element_type=jnp.float32)


def fold(s, vt, state, at, first=False):
    scale = math.log2(math.e) / math.sqrt(HEAD_SIZE)
    live = HEAD_SIZE + 8
    top = jnp.max(s, axis=0, keepdims=True)
    if not first:
        old = state[live : live + 1, at]
        top = jnp.maximum(old, top)
    p = jnp.exp2((s - top) * scale).astype(jnp.bfloat16)
    fresh = jnp.dot(vt, p, preferred_element_type=jnp.float32)[:live]
    if not first:
        fresh += state[:live, at] * jnp.exp2((old - top) * scale)
    state[:live, at] = fresh
    state[live : live + 1, at] = top


def fold_all(count, keys, values, queries, state):
    def some(first, n):
        s = scores(keys(first), queries(first))
        for i in range(n):
            now = s
            if i + 1 < n:
                s = scores(keys(first + i + 1), queries(first + i + 1))
            fold(now, values(first + i), *state(first + i))

    at_once = math.gcd(count, 4)

    def body(j, _):
        some(j * at_once, at_once)
        return 0

    lax.fori_loop(0, count // at_once, body, 0)


def values_and_ones(v, count=None):
    if count is not None:
        row = lax.broadcasted_iota(jnp.int32, v.shape, 0)
        v = jnp.where(row < count, v, jnp.zeros_like(v))
    n = v.shape[0]
    lane = lax.broadcasted_iota(jnp.int32, (SUMS - HEAD_SIZE, n), 1)
    row = lax.broadcasted_iota(jnp.int32, (SUMS - HEAD_SIZE, n), 0)
    live = row < 8
    if count is not None:
        live = live & (lane < count)
    ones = jnp.where(live, 1.0, 0.0).astype(jnp.bfloat16)
    return jnp.concatenate([v.T, ones], axis=0)


def attend_early(place, query, own, sets, after, name):
    rows = query.shape[0]
    kv_local = own.shape[1] // (2 * HEAD_SIZE)
    ratio = query.shape[1] // HEAD_SIZE // kv_local
    wide = ratio * TILE
    count = rows // TILE

    def columns(t):
        return pl.ds(pl.multiple_of(t * wide, 128), wide)

    def body(place_ref, q_ref, own_ref, *refs):
        out = refs[-1]
        for g in range(kv_local):
            base = g * 2 * HEAD_SIZE
            k = own_ref[:, base : base + HEAD_SIZE]
            vt = values_and_ones(own_ref[:, base + HEAD_SIZE : base + 2 * HEAD_SIZE])
            for t in range(count):
                upto = (t + 1) * TILE
                column = lax.broadcasted_iota(jnp.int32, (upto, wide), 1) % TILE + t * TILE
                key = lax.broadcasted_iota(jnp.int32, (upto, wide), 0)
                s = jnp.where(key <= column, scores(k[:upto], stacked(q_ref, t, ratio, g)), -1e30)
                fold(s, vt[:, :upto], out.at[g], slice(t * wide, (t + 1) * wide), first=True)
        if sets:
            k_ref, vt_ref = refs[:2]
            fold_all(
                kv_local * count,
                lambda i: k_ref[i // count],
                lambda i: vt_ref[i // count],
                lambda i: stacked(q_ref, i % count, ratio, i // count),
                lambda i: (out.at[i // count], columns(i % count)),
            )

    def whole(a):
        return pl.BlockSpec(a.shape, lambda i, place: (0,) * len(a.shape))

    args = [query, own, *[a for s in sets for a in s]]
    state_shape = jax.ShapeDtypeStruct((kv_local, SUMS, count * wide), jnp.float32)
    return pl.pallas_call(
        body,
        grid_spec=pltpu.PrefetchScalarGridSpec(
            num_scalar_prefetch=1,
            grid=(1,),
            in_specs=[whole(a) for a in args] + [ANY] * len(after),
            out_specs=whole(state_shape),
        ),
        out_shape=state_shape,
        name=name,
        cost_estimate=SMALL,
        compiler_params=pltpu.CompilerParams(vmem_limit_bytes=VMEM),
    )(place, *args, *after)


def attend_late(place, queries, states, arrived, rows, cache, start, total, last, after):
    kv_width = arrived[0].shape[1]
    kv_local = kv_width // (2 * HEAD_SIZE)
    ratio = queries[0].shape[1] // HEAD_SIZE // kv_local
    wide = ratio * TILE
    n_keys = sum(a.shape[0] for a in arrived)
    most = n_keys - rows
    tiles = sum(q.shape[0] for q in queries) // TILE
    firsts = [sum(q.shape[0] for q in queries[:i]) // TILE for i in range(len(queries))]
    n = len(queries)
    n_cache = 0 if cache is None else 1

    def body(place_ref, *refs):
        refs = list(refs)
        q_refs = [refs.pop(0) for _ in queries]
        state_refs = [refs.pop(0).at[0] for _ in states]
        arrived_refs = [refs.pop(0) for _ in arrived]
        for _ in range(n_cache + len(after)):
            refs.pop(0)
        cache_ref = refs.pop(0)
        if last:
            out = refs.pop(0)
            k_ref, vt_ref, kv, piece, sems, work, q_all = refs
        else:
            work = refs.pop(0).at[0]
            k_out, vt_out = refs.pop(0), refs.pop(0)
            k_ref, vt_ref, kv, piece, sems = refs
        g = pl.program_id(0)
        me, length, span = place_ref[0], place_ref[1], place_ref[2]
        count = me * rows

        def prepared(h, keys, count):
            base = h * 2 * HEAD_SIZE
            k = kv[:keys, base : base + HEAD_SIZE]
            row = lax.broadcasted_iota(jnp.int32, k.shape, 0)
            k = jnp.where(row < count, k, jnp.broadcast_to(k[:16][:1], k.shape))
            v = kv[:keys, base + HEAD_SIZE : base + 2 * HEAD_SIZE]
            return k, values_and_ones(v, count)

        def copies():
            return [
                pltpu.make_async_copy(
                    piece.at[j], cache_ref.at[j, pl.ds(start, rows), :], sems.at[j]
                )
                for j in range(GROUPS)
            ]

        @pl.when(g == 0)
        def _():
            def put(stretch, value):
                kv[pl.ds(pl.multiple_of(stretch * rows, 64), rows), :] = value

            if len(arrived) == 1:
                kv[:n_keys, :] = arrived_refs[0][...]
            else:
                half = len(arrived_refs) // 2
                for j, part in enumerate([arrived_refs[:half], arrived_refs[half:]]):
                    found = [
                        ref[i * rows : (i + 1) * rows, :]
                        for ref in part
                        for i in range(ref.shape[0] // rows)
                    ]
                    for i, block in enumerate(found):
                        put(me ^ (2 * i + j), block)
            for j in range(GROUPS):
                value = kv[pl.ds(pl.multiple_of((span + j) * rows, 64), rows), :]
                index = (span + j) * total + start
                index += lax.broadcasted_iota(jnp.int32, value.shape, 0)
                piece[j] = jnp.where(index < length, value, jnp.zeros_like(value))
            for c in copies():
                c.start()
            for h in range(kv_local):
                k_ref[h], vt_ref[h] = prepared(h, most, count)

        if last:
            q_ref, state = q_all, work
            for i, (q, s) in enumerate(zip(q_refs, state_refs)):
                q_all[firsts[i] * TILE : firsts[i] * TILE + q.shape[0], :] = q[...]
                state[:, firsts[i] * wide : firsts[i] * wide + s.shape[1]] = s[...]
        else:
            q_ref, state = q_refs[0], work
            state[...] = state_refs[0][...]

        @pl.when(count > 0)
        def _():
            fold_all(
                tiles,
                lambda i: k_ref[g],
                lambda i: vt_ref[g],
                lambda i: stacked(q_ref, i, ratio),
                lambda i: (state, pl.ds(pl.multiple_of(i * wide, 128), wide)),
            )

        if last:
            for i in range(tiles):
                at = slice(i * wide, (i + 1) * wide)
                done = (state[:HEAD_SIZE, at] / state[HEAD_SIZE : HEAD_SIZE + 1, at]).T
                for h in range(ratio):
                    out[i * TILE : (i + 1) * TILE, h * HEAD_SIZE : (h + 1) * HEAD_SIZE] = done[
                        h * TILE : (h + 1) * TILE
                    ].astype(jnp.bfloat16)
        else:
            for h in range(kv_local):

                @pl.when(g == h)
                def _():
                    k_out[0], vt_out[0] = prepared(h, n_keys, count + rows)


        @pl.when(g == kv_local - 1)
        def _():
            for c in copies():
                c.wait()

    def whole(a):
        return pl.BlockSpec(a.shape, lambda g, place: (0,) * len(a.shape))

    def by_group(a):
        return pl.BlockSpec((1,) + a.shape[1:], lambda g, place: (g,) + (0,) * (len(a.shape) - 1))

    k_shape = jax.ShapeDtypeStruct((kv_local, n_keys, HEAD_SIZE), jnp.bfloat16)
    vt_shape = jax.ShapeDtypeStruct((kv_local, SUMS, n_keys), jnp.bfloat16)
    cache_shape = jax.ShapeDtypeStruct((GROUPS, total, kv_width), jnp.bfloat16)
    args = [*queries, *states, *arrived]
    in_specs = [pl.BlockSpec((q.shape[0], ratio * HEAD_SIZE), lambda g, place: (0, g)) for q in queries]
    in_specs += [by_group(s) for s in states] + [whole(a) for a in arrived]
    aliases = {}
    if cache is not None:
        args.append(cache)
        in_specs.append(ANY)
        aliases[len(args)] = 0
    scratch = [
        pltpu.VMEM((kv_local, most, HEAD_SIZE), jnp.bfloat16),
        pltpu.VMEM((kv_local, SUMS, most), jnp.bfloat16),
        pltpu.VMEM((n_keys, kv_width), jnp.bfloat16),
        pltpu.VMEM((GROUPS, rows, kv_width), jnp.bfloat16),
        pltpu.SemaphoreType.DMA((GROUPS,)),
    ]
    if last:
        out_shape = [cache_shape, jax.ShapeDtypeStruct((total, queries[0].shape[1]), jnp.bfloat16)]
        out_specs = [ANY, pl.BlockSpec((total, ratio * HEAD_SIZE), lambda g, place: (0, g))]
        scratch += [
            pltpu.VMEM((SUMS, tiles * wide), jnp.float32),
            pltpu.VMEM((tiles * TILE, ratio * HEAD_SIZE), jnp.bfloat16),
        ]
    else:
        out_shape = [cache_shape, *[jax.ShapeDtypeStruct(s.shape, s.dtype) for s in states]]
        out_shape += [k_shape, vt_shape]
        out_specs = [ANY] + [by_group(s) for s in out_shape[1:]]
        for i in range(n):
            aliases[1 + n + i] = 1 + i
    return pl.pallas_call(
        body,
        grid_spec=pltpu.PrefetchScalarGridSpec(
            num_scalar_prefetch=1,
            grid=(kv_local,),
            in_specs=in_specs + [ANY] * len(after),
            out_specs=out_specs,
            scratch_shapes=scratch,
        ),
        out_shape=out_shape,
        input_output_aliases=aliases,
        name=f"late_{start}",
        cost_estimate=SMALL,
        compiler_params=pltpu.CompilerParams(vmem_limit_bytes=VMEM),
    )(place, *args, *after)


def pack(blocks, after, name):
    rows = blocks[0].shape[0]

    def body(*refs):
        for i in range(len(blocks)):
            refs[-1][i * rows : (i + 1) * rows, :] = refs[i][...]

    spec = pl.BlockSpec(memory_space=pltpu.VMEM)
    shape = (rows * len(blocks), blocks[0].shape[1])
    return pl.pallas_call(
        body,
        in_specs=[spec] * len(blocks) + [ANY] * len(after),
        out_specs=spec,
        out_shape=jax.ShapeDtypeStruct(shape, blocks[0].dtype),
        cost_estimate=SMALL,
        name=name,
    )(*blocks, *after)


def exchange(x, after, name, pieces=1):
    even = [x] + [paired(x, "chain", mask) for mask in range(2, lax.axis_size("chain"), 2)]
    size = len(even) // pieces
    even = [
        pack(even[i * size : (i + 1) * size], after, f"{name}_{i}") for i in range(pieces)
    ]
    return (*even, *[paired(e, "chain", 1) for e in even])


def local(tokens, gain, w_query, key_value_weight, offsets, lengths):
    rows = tokens.shape[0]
    kv_local = key_value_weight.shape[1] // (2 * HEAD_SIZE)
    me = lax.axis_index("chain")
    chain = lax.axis_size("chain")
    tp = lax.axis_size("tp")
    lane = lax.axis_index("tp")

    half = HEAD_SIZE // 2
    freq = jnp.power(
        jnp.float32(500000.0), -2.0 * jnp.arange(half).astype(jnp.float32) / HEAD_SIZE
    )
    position = offsets[0] + jnp.arange(rows, dtype=jnp.int32)
    angle = position.astype(jnp.float32)[:, None] * freq[None, :]
    cosine, sine = jnp.cos(angle), jnp.sin(angle)
    cosine = jnp.concatenate([cosine, cosine], axis=1)
    sine = jnp.concatenate([-sine, sine], axis=1)

    members = chain // GROUPS
    span = me % members * GROUPS
    length = jnp.sum(jnp.where(jnp.arange(GROUPS) == me // members, lengths, 0))
    place = jnp.stack([me, length, span]).astype(jnp.int32)

    sizes = [rows * FIRST // 8, rows * (8 - FIRST) // 8]
    starts = [0, sizes[0]]
    weights = (w_query, key_value_weight)
    arrived = [None] * len(sizes)

    def send(r, after):
        chunk = cut(tokens, starts[r], sizes[r], after, f"cut_{r}")
        if tp == 4:
            arrived[r] = [chunk, shifted(chunk, "tp", 1), shifted(chunk, "tp", -1)]
        else:
            arrived[r] = [lax.all_gather(chunk, "tp", axis=0)]
        return chunk

    def forward(r, i, after):
        if tp != 4:
            return arrived[r][0]
        half = sizes[r] // 2
        part = cut(arrived[r][i], (i - 1) * half, half, after, f"pass_{r}_{i}")
        arrived[r].append(shifted(part, "tp", 3 - 2 * i))
        return part

    def near(r, after):
        if tp == 4:
            parts, which, carry = arrived[r][1:3], order[1:3], (own, starts[r])
        else:
            parts, which, carry = [arrived[r][0][i] for i in range(tp - 1)], order[:-1], None
        return add_products(parts, which, gain, weights, carry, 1024, after, f"near_{r}")

    def finish(r, weight, turned, sums, squares, after, name):
        part = arrived[r][3:] if tp == 4 else [arrived[r][0][tp - 1]]
        at = slice(starts[r], starts[r] + sizes[r])
        tables = (cosine[at], sine[at])
        return finish_products(
            part, order[-1:], gain, weight, turned, sums, squares, tables, after, f"{name}_{r}"
        )

    def keys_and_queries(r, sums, after=()):
        q_sums, kv_sums, squares = sums
        kv = finish(r, key_value_weight, (True, False), kv_sums, squares, after, "kv")
        query = finish(r, w_query, (True, True), q_sums, squares, (kv,), "query")
        return kv, query

    if tp == 4:
        order = jnp.stack([lane, (lane + 3) % 4, (lane + 1) % 4, (lane + 2) % 4])
        order = order.astype(jnp.int32)
    else:
        order = jnp.arange(tp, dtype=jnp.int32)

    step = send(0, ())
    if tp == 4:
        own = add_products([tokens], order[:1], gain, weights, None, 1024, (step,), "own")
        step = own[-1]
    step = forward(0, 1, (step,))
    step = forward(0, 2, (step,))
    sums = near(0, (step,))
    step = send(1, (sums[2],))
    kv_0, query_0 = keys_and_queries(0, sums, (step,))
    keys = exchange(kv_0, (query_0,), "pack_0", 2)
    state_0 = attend_early(place, query_0, kv_0, [], keys[:1], "early_0")
    step = forward(1, 1, (state_0,))
    cache, state_0, k, vt = attend_late(
        place, [query_0], [state_0], keys, sizes[0], None, 0, rows, False, (step,)
    )
    step = forward(1, 2, (k,))
    sums = near(1, (step,))
    kv_1, query_1 = keys_and_queries(1, sums)
    keys = exchange(kv_1, (query_1,), "pack_1")
    state_1 = attend_early(place, query_1, kv_1, [(k, vt)], keys[:1], "early_1")
    queries, states = [query_0, query_1], [state_0, state_1]
    cache, context = attend_late(
        place, queries, states, keys, sizes[1], cache, starts[1], rows, True, ()
    )
    return context, cache.reshape(GROUPS * rows, key_value_weight.shape[1])


def solution(mesh):
    in_specs = (P("chain", "tp"), P(), P(None, "tp"), P(None, "tp"), P("chain"), P())
    out_specs = (P("chain", "tp"), P("chain", "tp"))
    return jax.shard_map(local, mesh=mesh, in_specs=in_specs, out_specs=out_specs, check_vma=False)
```

```python
import math

import jax
import jax.numpy as jnp
from jax import lax
from jax.experimental import pallas as pl
from jax.experimental.pallas import tpu as pltpu
from jax.sharding import PartitionSpec as P

HEAD_SIZE = 128
GROUPS = 4
TILE = 64
FIRST = 4
SUMS = HEAD_SIZE + 16
VMEM = 63 * 1024 * 1024
SMALL = pl.CostEstimate(flops=1000, bytes_accessed=1000, transcendentals=0)
ANY = pl.BlockSpec(memory_space=pl.ANY)


def shifted(x, axis, by):
    n = lax.axis_size(axis)
    return lax.ppermute(x, axis, [(i, (i + by) % n) for i in range(n)])


def paired(x, axis, mask):
    return lax.ppermute(x, axis, [(i, i ^ mask) for i in range(lax.axis_size(axis))])


def cut(x, start, rows, after, name):
    def body(x_ref, *refs):
        out, held, sems = refs[-3:]
        for i, (a, b) in enumerate([(x_ref.at[pl.ds(start, rows), :], held), (held, out)]):
            copy = pltpu.make_async_copy(a, b, sems.at[i])
            copy.start()
            copy.wait()

    return pl.pallas_call(
        body,
        in_specs=[pl.BlockSpec(memory_space=pltpu.HBM)] + [ANY] * len(after),
        out_specs=pl.BlockSpec(memory_space=pltpu.HBM),
        out_shape=jax.ShapeDtypeStruct((rows, x.shape[1]), x.dtype),
        scratch_shapes=[
            pltpu.VMEM((rows, x.shape[1]), x.dtype),
            pltpu.SemaphoreType.DMA((2,)),
        ],
        cost_estimate=SMALL,
        name=name,
    )(x, *after)


def normed_rows(parts_refs, gain_ref, x_ref, square_ref):
    at = 0
    for ref in parts_refs:
        rows = slice(at, at + ref.shape[0])
        x = ref[...].astype(jnp.float32)
        x_ref[rows, :] = (x * gain_ref[0]).astype(jnp.bfloat16)
        square = x * x
        square_ref[rows, :] += sum(square[:, i : i + 128] for i in range(0, x.shape[1], 128))
        at += ref.shape[0]


def add_products(parts, order, gain, weights, carry, depth, after, name):
    count = len(parts)
    rows, width = parts[0].shape
    pieces = rows // TILE
    depth = min(depth, width)
    steps = width // depth
    model = weights[0].shape[0]
    n = len(weights)

    def body(order_ref, *refs):
        refs = list(refs)
        part_refs = [refs.pop(0) for _ in parts]
        gain_ref = refs.pop(0)
        w_refs = [refs.pop(0) for _ in weights]
        carry_refs = [[refs.pop(0) for _ in range(pieces)] for _ in range(n + 1)] if carry else None
        *sums, x_ref = refs[len(after) :]
        step = pl.program_id(0)

        @pl.when(step == 0)
        def _():
            for i, s in enumerate(sums):
                if carry:
                    for piece, ref in enumerate(carry_refs[i]):
                        s[piece * TILE : (piece + 1) * TILE, :] = ref[...]
                else:
                    s[...] = jnp.zeros_like(s)

        for i in range(count):

            @pl.when(step // steps == i)
            def _():
                normed_rows([part_refs[i]], gain_ref, x_ref, sums[-1])

        for s, w in zip(sums, w_refs):
            wide = w.shape[1] if carry else math.gcd(w.shape[1], 512)

            def add(i, _, s=s, w=w, wide=wide):
                at = pl.ds(pl.multiple_of(i * wide, 128), wide)
                s[:, at] += jnp.dot(x_ref[...], w[:, at], preferred_element_type=jnp.float32)
                return 0

            lax.fori_loop(0, w.shape[1] // wide, add, 0)

    def part_spec(i):
        return pl.BlockSpec(
            (rows, depth), lambda s, order: (0, jnp.clip(s - i * steps, 0, steps - 1))
        )

    def carry_spec(columns, piece):
        return pl.BlockSpec((TILE, columns), lambda s, order: (carry[1] // TILE + piece, 0))

    def block(s, order):
        return order[s // steps] * steps + s % steps

    columns = [w.shape[1] for w in weights]
    out_shape = [jax.ShapeDtypeStruct((rows, c), jnp.float32) for c in (*columns, 128)]
    in_specs = [part_spec(i) for i in range(count)]
    in_specs += [pl.BlockSpec((1, 1, depth), lambda s, order: (block(s, order), 0, 0))]
    in_specs += [
        pl.BlockSpec((depth, c), lambda s, order: (block(s, order), 0)) for c in columns
    ]
    if carry:
        in_specs += [carry_spec(s.shape[1], p) for s in out_shape for p in range(pieces)]
    return pl.pallas_call(
        body,
        grid_spec=pltpu.PrefetchScalarGridSpec(
            num_scalar_prefetch=1,
            grid=(count * steps,),
            in_specs=in_specs + [ANY] * len(after),
            out_specs=[pl.BlockSpec(s.shape, lambda s, order: (0, 0)) for s in out_shape],
            scratch_shapes=[pltpu.VMEM((rows, depth), jnp.bfloat16)],
        ),
        out_shape=out_shape,
        name=name,
        cost_estimate=SMALL,
        compiler_params=pltpu.CompilerParams(vmem_limit_bytes=VMEM),
    )(
        order,
        *parts,
        gain.reshape(model // depth, 1, depth),
        *weights,
        *([a for a in carry[0] for _ in range(pieces)] if carry else ()),
        *after,
    )


def finish_products(part, order, gain, weight, turned, sums, squares, tables, after, name):
    width = part[0].shape[1]
    rows = sum(p.shape[0] for p in part)
    model, columns = weight.shape
    wide = min(columns, 1024)

    def body(order_ref, *refs):
        refs = list(refs)
        part_refs = [refs.pop(0) for _ in part]
        gain_ref, w_ref, sums_ref, squares_ref, cosine_ref, sine_ref = refs[:6]
        out, x_ref, square_ref = refs[-3:]

        @pl.when(pl.program_id(0) == 0)
        def _():
            square_ref[...] = squares_ref[...]
            normed_rows(part_refs, gain_ref, x_ref, square_ref)
            total = jnp.sum(square_ref[...], axis=1, keepdims=True)
            square_ref[...] = jnp.broadcast_to(lax.rsqrt(total / model + 1e-05), square_ref.shape)

        inv = square_ref[...]
        sums = sums_ref[...] + jnp.dot(x_ref[...], w_ref[...], preferred_element_type=jnp.float32)
        for i, at in enumerate(range(0, wide, 128)):
            u = sums[:, at : at + 128] * inv
            if turned[i % 2]:
                u = u * cosine_ref[...] + pltpu.roll(u, 64, 1) * sine_ref[...]
            out[:, at : at + 128] = u.astype(jnp.bfloat16)

    def whole(a):
        return pl.BlockSpec(a.shape, lambda s, order: (0, 0))

    by_columns = pl.BlockSpec((rows, wide), lambda s, order: (0, s))
    return pl.pallas_call(
        body,
        grid_spec=pltpu.PrefetchScalarGridSpec(
            num_scalar_prefetch=1,
            grid=(columns // wide,),
            in_specs=[whole(p) for p in part]
            + [pl.BlockSpec((1, 1, width), lambda s, order: (order[0], 0, 0))]
            + [pl.BlockSpec((width, wide), lambda s, order: (order[0], s))]
            + [by_columns, whole(squares), whole(tables[0]), whole(tables[1])]
            + [ANY] * len(after),
            out_specs=by_columns,
            scratch_shapes=[
                pltpu.VMEM((rows, width), jnp.bfloat16),
                pltpu.VMEM((rows, 128), jnp.float32),
            ],
        ),
        out_shape=jax.ShapeDtypeStruct((rows, columns), jnp.bfloat16),
        name=name,
        cost_estimate=SMALL,
        compiler_params=pltpu.CompilerParams(vmem_limit_bytes=VMEM),
    )(order, *part, gain.reshape(model // width, 1, width), weight, sums, squares, *tables, *after)


def stacked(q_ref, tile, ratio, group=0):
    rows = pl.ds(pl.multiple_of(tile * TILE, TILE), TILE)
    return jnp.concatenate(
        [
            q_ref[rows, pl.ds(pl.multiple_of((group * ratio + h) * HEAD_SIZE, HEAD_SIZE), HEAD_SIZE)]
            for h in range(ratio)
        ],
        axis=0,
    )


def scores(k, q):
    return lax.dot_general(k, q, (((1,), (1,)), ((), ())), preferred_element_type=jnp.float32)


def fold(s, vt, state, at, first=False):
    scale = math.log2(math.e) / math.sqrt(HEAD_SIZE)
    live = HEAD_SIZE + 8
    top = jnp.max(s, axis=0, keepdims=True)
    if not first:
        old = state[live : live + 1, at]
        top = jnp.maximum(old, top)
    p = jnp.exp2((s - top) * scale).astype(jnp.bfloat16)
    fresh = jnp.dot(vt, p, preferred_element_type=jnp.float32)[:live]
    if not first:
        fresh += state[:live, at] * jnp.exp2((old - top) * scale)
    state[:live, at] = fresh
    state[live : live + 1, at] = top


def fold_all(count, at_once, keys, values, queries, state):
    def some(first, n):
        s = scores(keys(first), queries(first))
        for i in range(n):
            now = s
            if i + 1 < n:
                s = scores(keys(first + i + 1), queries(first + i + 1))
            fold(now, values(first + i), *state(first + i))

    at_once = math.gcd(count, at_once)
    if at_once == count:
        some(0, count)
        return

    def body(j, _):
        some(j * at_once, at_once)
        return 0

    lax.fori_loop(0, count // at_once, body, 0)


def values_and_ones(v, count=None):
    if count is not None:
        row = lax.broadcasted_iota(jnp.int32, v.shape, 0)
        v = jnp.where(row < count, v, jnp.zeros_like(v))
    n = v.shape[0]
    lane = lax.broadcasted_iota(jnp.int32, (SUMS - HEAD_SIZE, n), 1)
    row = lax.broadcasted_iota(jnp.int32, (SUMS - HEAD_SIZE, n), 0)
    live = row < 8
    if count is not None:
        live = live & (lane < count)
    ones = jnp.where(live, 1.0, 0.0).astype(jnp.bfloat16)
    return jnp.concatenate([v.T, ones], axis=0)


def attend_early(place, query, own, sets, after, name):
    rows = query.shape[0]
    kv_local = own.shape[1] // (2 * HEAD_SIZE)
    ratio = query.shape[1] // HEAD_SIZE // kv_local
    wide = ratio * TILE
    count = rows // TILE

    def columns(t):
        return pl.ds(pl.multiple_of(t * wide, 128), wide)

    def body(place_ref, q_ref, own_ref, *refs):
        out = refs[-1]
        for g in range(kv_local):
            base = g * 2 * HEAD_SIZE
            k = own_ref[:, base : base + HEAD_SIZE]
            vt = values_and_ones(own_ref[:, base + HEAD_SIZE : base + 2 * HEAD_SIZE])
            for t in range(count):
                upto = (t + 1) * TILE
                column = lax.broadcasted_iota(jnp.int32, (upto, wide), 1) % TILE + t * TILE
                key = lax.broadcasted_iota(jnp.int32, (upto, wide), 0)
                s = jnp.where(key <= column, scores(k[:upto], stacked(q_ref, t, ratio, g)), -1e30)
                fold(s, vt[:, :upto], out.at[g], slice(t * wide, (t + 1) * wide), first=True)
        if sets:
            k_ref, vt_ref = refs[:2]
            fold_all(
                kv_local * count,
                4,
                lambda i: k_ref[i // count],
                lambda i: vt_ref[i // count],
                lambda i: stacked(q_ref, i % count, ratio, i // count),
                lambda i: (out.at[i // count], columns(i % count)),
            )

    def whole(a):
        return pl.BlockSpec(a.shape, lambda i, place: (0,) * len(a.shape))

    args = [query, own, *[a for s in sets for a in s]]
    state_shape = jax.ShapeDtypeStruct((kv_local, SUMS, count * wide), jnp.float32)
    return pl.pallas_call(
        body,
        grid_spec=pltpu.PrefetchScalarGridSpec(
            num_scalar_prefetch=1,
            grid=(1,),
            in_specs=[whole(a) for a in args] + [ANY] * len(after),
            out_specs=whole(state_shape),
        ),
        out_shape=state_shape,
        name=name,
        cost_estimate=SMALL,
        compiler_params=pltpu.CompilerParams(vmem_limit_bytes=VMEM),
    )(place, *args, *after)


def attend_late(place, queries, states, arrived, rows, cache, start, total, last, after):
    kv_width = arrived[0].shape[1]
    kv_local = kv_width // (2 * HEAD_SIZE)
    ratio = queries[0].shape[1] // HEAD_SIZE // kv_local
    wide = ratio * TILE
    n_keys = sum(a.shape[0] for a in arrived)
    most = n_keys - rows
    tiles = sum(q.shape[0] for q in queries) // TILE
    firsts = [sum(q.shape[0] for q in queries[:i]) // TILE for i in range(len(queries))]
    n = len(queries)
    n_cache = 0 if cache is None else 1

    def body(place_ref, *refs):
        refs = list(refs)
        q_refs = [refs.pop(0) for _ in queries]
        state_refs = [refs.pop(0).at[0] for _ in states]
        arrived_refs = [refs.pop(0) for _ in arrived]
        for _ in range(n_cache + len(after)):
            refs.pop(0)
        cache_ref = refs.pop(0)
        if last:
            out = refs.pop(0)
            k_ref, vt_ref, kv, piece, sems, work, q_all = refs
        else:
            work = refs.pop(0).at[0]
            k_out, vt_out = refs.pop(0), refs.pop(0)
            k_ref, vt_ref, kv, piece, sems = refs
        g = pl.program_id(0)
        me, length, span = place_ref[0], place_ref[1], place_ref[2]
        count = me * rows

        def prepared(h, keys, count):
            base = h * 2 * HEAD_SIZE
            k = kv[:keys, base : base + HEAD_SIZE]
            row = lax.broadcasted_iota(jnp.int32, k.shape, 0)
            k = jnp.where(row < count, k, jnp.broadcast_to(k[:16][:1], k.shape))
            v = kv[:keys, base + HEAD_SIZE : base + 2 * HEAD_SIZE]
            return k, values_and_ones(v, count)

        def copies():
            return [
                pltpu.make_async_copy(
                    piece.at[j], cache_ref.at[j, pl.ds(start, rows), :], sems.at[j]
                )
                for j in range(GROUPS)
            ]

        @pl.when(g == 0)
        def _():
            def put(stretch, value):
                kv[pl.ds(pl.multiple_of(stretch * rows, 64), rows), :] = value

            if len(arrived) == 1:
                kv[:n_keys, :] = arrived_refs[0][...]
            else:
                half = len(arrived_refs) // 2
                for j, part in enumerate([arrived_refs[:half], arrived_refs[half:]]):
                    found = [
                        ref[i * rows : (i + 1) * rows, :]
                        for ref in part
                        for i in range(ref.shape[0] // rows)
                    ]
                    for i, block in enumerate(found):
                        put(me ^ (2 * i + j), block)
            for j in range(GROUPS):
                value = kv[pl.ds(pl.multiple_of((span + j) * rows, 64), rows), :]
                index = (span + j) * total + start
                index += lax.broadcasted_iota(jnp.int32, value.shape, 0)
                piece[j] = jnp.where(index < length, value, jnp.zeros_like(value))
            for c in copies():
                c.start()
            for h in range(kv_local):
                k_ref[h], vt_ref[h] = prepared(h, most, count)

        if last:
            q_ref, state = q_all, work
            for i, (q, s) in enumerate(zip(q_refs, state_refs)):
                q_all[firsts[i] * TILE : firsts[i] * TILE + q.shape[0], :] = q[...]
                state[:, firsts[i] * wide : firsts[i] * wide + s.shape[1]] = s[...]
        else:
            q_ref, state = q_refs[0], work
            state[...] = state_refs[0][...]

        @pl.when(count > 0)
        def _():
            fold_all(
                tiles,
                8,
                lambda i: k_ref[g],
                lambda i: vt_ref[g],
                lambda i: stacked(q_ref, i, ratio),
                lambda i: (state, pl.ds(pl.multiple_of(i * wide, 128), wide)),
            )

        if last:
            for i in range(tiles):
                at = slice(i * wide, (i + 1) * wide)
                done = (state[:HEAD_SIZE, at] / state[HEAD_SIZE : HEAD_SIZE + 1, at]).T
                for h in range(ratio):
                    out[i * TILE : (i + 1) * TILE, h * HEAD_SIZE : (h + 1) * HEAD_SIZE] = done[
                        h * TILE : (h + 1) * TILE
                    ].astype(jnp.bfloat16)
        else:
            for h in range(kv_local):

                @pl.when(g == h)
                def _():
                    k_out[0], vt_out[0] = prepared(h, n_keys, count + rows)


        @pl.when(g == kv_local - 1)
        def _():
            for c in copies():
                c.wait()

    def whole(a):
        return pl.BlockSpec(a.shape, lambda g, place: (0,) * len(a.shape))

    def by_group(a):
        return pl.BlockSpec((1,) + a.shape[1:], lambda g, place: (g,) + (0,) * (len(a.shape) - 1))

    k_shape = jax.ShapeDtypeStruct((kv_local, n_keys, HEAD_SIZE), jnp.bfloat16)
    vt_shape = jax.ShapeDtypeStruct((kv_local, SUMS, n_keys), jnp.bfloat16)
    cache_shape = jax.ShapeDtypeStruct((GROUPS, total, kv_width), jnp.bfloat16)
    args = [*queries, *states, *arrived]
    in_specs = [pl.BlockSpec((q.shape[0], ratio * HEAD_SIZE), lambda g, place: (0, g)) for q in queries]
    in_specs += [by_group(s) for s in states] + [whole(a) for a in arrived]
    aliases = {}
    if cache is not None:
        args.append(cache)
        in_specs.append(ANY)
        aliases[len(args)] = 0
    scratch = [
        pltpu.VMEM((kv_local, most, HEAD_SIZE), jnp.bfloat16),
        pltpu.VMEM((kv_local, SUMS, most), jnp.bfloat16),
        pltpu.VMEM((n_keys, kv_width), jnp.bfloat16),
        pltpu.VMEM((GROUPS, rows, kv_width), jnp.bfloat16),
        pltpu.SemaphoreType.DMA((GROUPS,)),
    ]
    if last:
        out_shape = [cache_shape, jax.ShapeDtypeStruct((total, queries[0].shape[1]), jnp.bfloat16)]
        out_specs = [ANY, pl.BlockSpec((total, ratio * HEAD_SIZE), lambda g, place: (0, g))]
        scratch += [
            pltpu.VMEM((SUMS, tiles * wide), jnp.float32),
            pltpu.VMEM((tiles * TILE, ratio * HEAD_SIZE), jnp.bfloat16),
        ]
    else:
        out_shape = [cache_shape, *[jax.ShapeDtypeStruct(s.shape, s.dtype) for s in states]]
        out_shape += [k_shape, vt_shape]
        out_specs = [ANY] + [by_group(s) for s in out_shape[1:]]
        for i in range(n):
            aliases[1 + n + i] = 1 + i
    return pl.pallas_call(
        body,
        grid_spec=pltpu.PrefetchScalarGridSpec(
            num_scalar_prefetch=1,
            grid=(kv_local,),
            in_specs=in_specs + [ANY] * len(after),
            out_specs=out_specs,
            scratch_shapes=scratch,
        ),
        out_shape=out_shape,
        input_output_aliases=aliases,
        name=f"late_{start}",
        cost_estimate=SMALL,
        compiler_params=pltpu.CompilerParams(vmem_limit_bytes=VMEM),
    )(place, *args, *after)


def pack(blocks, after, name):
    rows = blocks[0].shape[0]

    def body(*refs):
        for i in range(len(blocks)):
            refs[-1][i * rows : (i + 1) * rows, :] = refs[i][...]

    spec = pl.BlockSpec(memory_space=pltpu.VMEM)
    shape = (rows * len(blocks), blocks[0].shape[1])
    return pl.pallas_call(
        body,
        in_specs=[spec] * len(blocks) + [ANY] * len(after),
        out_specs=spec,
        out_shape=jax.ShapeDtypeStruct(shape, blocks[0].dtype),
        cost_estimate=SMALL,
        name=name,
    )(*blocks, *after)


def exchange(x, after, name, pieces=1):
    even = [x] + [paired(x, "chain", mask) for mask in range(2, lax.axis_size("chain"), 2)]
    size = len(even) // pieces
    even = [
        pack(even[i * size : (i + 1) * size], after, f"{name}_{i}") for i in range(pieces)
    ]
    return (*even, *[paired(e, "chain", 1) for e in even])


def local(tokens, gain, w_query, key_value_weight, offsets, lengths):
    rows = tokens.shape[0]
    kv_local = key_value_weight.shape[1] // (2 * HEAD_SIZE)
    me = lax.axis_index("chain")
    chain = lax.axis_size("chain")
    tp = lax.axis_size("tp")
    lane = lax.axis_index("tp")

    half = HEAD_SIZE // 2
    freq = jnp.power(
        jnp.float32(500000.0), -2.0 * jnp.arange(half).astype(jnp.float32) / HEAD_SIZE
    )
    position = offsets[0] + jnp.arange(rows, dtype=jnp.int32)
    angle = position.astype(jnp.float32)[:, None] * freq[None, :]
    cosine, sine = jnp.cos(angle), jnp.sin(angle)
    cosine = jnp.concatenate([cosine, cosine], axis=1)
    sine = jnp.concatenate([-sine, sine], axis=1)

    members = chain // GROUPS
    span = me % members * GROUPS
    length = jnp.sum(jnp.where(jnp.arange(GROUPS) == me // members, lengths, 0))
    place = jnp.stack([me, length, span]).astype(jnp.int32)

    sizes = [rows * FIRST // 8, rows * (8 - FIRST) // 8]
    starts = [0, sizes[0]]
    weights = (w_query, key_value_weight)
    arrived = [None] * len(sizes)

    def send(r, after):
        chunk = cut(tokens, starts[r], sizes[r], after, f"cut_{r}")
        if tp == 4:
            arrived[r] = [chunk, shifted(chunk, "tp", 1), shifted(chunk, "tp", -1)]
        else:
            arrived[r] = [lax.all_gather(chunk, "tp", axis=0)]
        return chunk

    def forward(r, i, after):
        if tp != 4:
            return arrived[r][0]
        half = sizes[r] // 2
        part = cut(arrived[r][i], (i - 1) * half, half, after, f"pass_{r}_{i}")
        arrived[r].append(shifted(part, "tp", 3 - 2 * i))
        return part

    def near(r, after):
        if tp == 4:
            parts, which, carry = arrived[r][1:3], order[1:3], (own, starts[r])
        else:
            parts, which, carry = [arrived[r][0][i] for i in range(tp - 1)], order[:-1], None
        return add_products(parts, which, gain, weights, carry, 1024, after, f"near_{r}")

    def finish(r, weight, turned, sums, squares, after, name):
        part = arrived[r][3:] if tp == 4 else [arrived[r][0][tp - 1]]
        at = slice(starts[r], starts[r] + sizes[r])
        tables = (cosine[at], sine[at])
        return finish_products(
            part, order[-1:], gain, weight, turned, sums, squares, tables, after, f"{name}_{r}"
        )

    def keys_and_queries(r, sums, after=()):
        q_sums, kv_sums, squares = sums
        kv = finish(r, key_value_weight, (True, False), kv_sums, squares, after, "kv")
        query = finish(r, w_query, (True, True), q_sums, squares, (kv,), "query")
        return kv, query

    if tp == 4:
        order = jnp.stack([lane, (lane + 3) % 4, (lane + 1) % 4, (lane + 2) % 4])
        order = order.astype(jnp.int32)
    else:
        order = jnp.arange(tp, dtype=jnp.int32)

    step = send(0, ())
    if tp == 4:
        own = add_products([tokens], order[:1], gain, weights, None, 1024, (step,), "own")
        step = own[-1]
    step = forward(0, 1, (step,))
    step = forward(0, 2, (step,))
    sums = near(0, (step,))
    step = send(1, (sums[2],))
    kv_0, query_0 = keys_and_queries(0, sums, (step,))
    keys = exchange(kv_0, (query_0,), "pack_0", 2)
    state_0 = attend_early(place, query_0, kv_0, [], keys[:1], "early_0")
    step = forward(1, 1, (state_0,))
    cache, state_0, k, vt = attend_late(
        place, [query_0], [state_0], keys, sizes[0], None, 0, rows, False, (step,)
    )
    step = forward(1, 2, (k,))
    sums = near(1, (step,))
    kv_1, query_1 = keys_and_queries(1, sums)
    keys = exchange(kv_1, (query_1,), "pack_1")
    state_1 = attend_early(place, query_1, kv_1, [(k, vt)], keys[:1], "early_1")
    queries, states = [query_0, query_1], [state_0, state_1]
    cache, context = attend_late(
        place, queries, states, keys, sizes[1], cache, starts[1], rows, True, ()
    )
    return context, cache.reshape(GROUPS * rows, key_value_weight.shape[1])


def solution(mesh):
    in_specs = (P("chain", "tp"), P(), P(None, "tp"), P(None, "tp"), P("chain"), P())
    out_specs = (P("chain", "tp"), P("chain", "tp"))
    return jax.shard_map(local, mesh=mesh, in_specs=in_specs, out_specs=out_specs, check_vma=False)
```
